256 devices in a mesh: frame: 32 (over z_lo, x, core), row: 8 (over y, z_hi).
Axes of the slice: x: 4, y: 4, z: 8 (z_hi: 2, z_lo: 4; z = z_hi * 4 + z_lo), core: 2. Of those that a mesh axis runs over, the one named last changes fastest.
Arguments:
- frames: bfloat16 [32, 32, 384, 128], P('frame', 'row'), may hold values from -20 to 20
- norm_gain: float32 [128], replicated, may hold values from 0.5 to 1.5
- qkv_weight: bfloat16 [3, 128, 128], replicated, may hold values from -12 to 12
- out_weight: bfloat16 [128, 128], replicated, may hold values from -0.5 to 0.5
- conv_weight: bfloat16 [3, 3, 128, 128], replicated, may hold values from -0.1875 to 0.1875
- out_grad: bfloat16 [32, 32, 384, 128], P('frame', 'row'), may hold values from -6 to 6
Outputs:
- output: bfloat16 [32, 32, 384, 128], P('frame', 'row')
- grad_frames: bfloat16 [32, 32, 384, 128], P('frame', 'row')
- grad_gain: float32 [128], replicated
- grad_qkv: float32 [3, 128, 128], replicated
- grad_out: float32 [128, 128], replicated
- grad_conv: float32 [3, 3, 128, 128], replicated
The draws below stay inside these ranges and needn't reach their ends.
All inputs are finite; a program needn't handle non-finite values.
Results may differ from the reference program's by a relative error of at most 0.013.
The reference program's roundings to bfloat16 on the way count: a program that leaves them out, or rounds other values in their place, can miss the bound.
Values may be sent and summed in bfloat16 or wider, within the bound.
A program may use at most 64 MiB of HBM per device.

```python
import math
import jax
import jax.numpy as jnp
from jax import lax

C = 128
HEADS = 4
IMG_W = 384
FRAMES = 32
IMG_H = 32


def draw_frames(key, part):
    key = jax.random.fold_in(key, 11)
    shape = (FRAMES, IMG_H, IMG_W, C)
    values = jnp.clip(jax.random.normal(key, shape, jnp.float32), -6.0, 6.0)
    return values.astype(jnp.bfloat16)


def draw_qkv_weight(key, part):
    key = jax.random.fold_in(key, 23)
    base_key = jax.random.fold_in(key, 0)
    base = jnp.clip(jax.random.normal(base_key, (3, C, C), jnp.float32), -4.0, 4.0) * C ** (-0.5)
    return base.astype(jnp.bfloat16)


def shard_levels(stream_key, dims, cuts, low, largest):
    factor_of, own = 1.0, jax.random.fold_in(stream_key, 6)
    for axis_at, parts in cuts:
        heights = jnp.exp(jax.random.uniform(jax.random.fold_in(own, axis_at), (parts,), jnp.float32, low / len(cuts), largest / len(cuts)))
        factor_of = factor_of * jnp.repeat(heights, dims[axis_at] // parts).reshape([-1 if axis == axis_at else 1 for axis in range(len(dims))])
    return factor_of


def scatter_about(own_key, extent, scale, bound, cuts=(), kind=jnp.bfloat16):
    entries = scale * jax.random.normal(own_key, extent, jnp.float32)
    if cuts:
        entries = entries * shard_levels(own_key, extent, cuts, -0.22, 0.18)
    return jnp.clip(entries, -bound, bound).astype(kind)


def setup_inputs(seed: int = 0) -> dict:
    splits = jax.random.split(jax.random.key(seed), 7)
    return {
        "frames": draw_frames(jax.random.fold_in(splits[6], 71), 0),
        "norm_gain": jnp.clip(1.0 + 0.1 * jax.random.normal(splits[1], (C,), jnp.float32), 0.5, 1.5),
        "qkv_weight": draw_qkv_weight(jax.random.fold_in(splits[6], 71), 0),
        "out_weight": scatter_about(splits[3], (C, C), C ** -0.5, 0.5),
        "conv_weight": scatter_about(splits[4], (3, 3, C, C), (9 * C) ** -0.5, 0.1875),
        "out_grad": scatter_about(splits[5], (FRAMES, IMG_H, IMG_W, C), 1.0, 6.0, ((0, 32), (1, 8))),
    }


EPSILON = 1e-05

def normalize(frames, norm_gain):
    values = frames.astype(jnp.float32)
    center = lax.optimization_barrier(jnp.mean(values, axis=-1, keepdims=True))
    spread = lax.optimization_barrier(jnp.mean(jnp.square(values - center), axis=-1, keepdims=True))
    inverse = lax.rsqrt(spread + EPSILON)
    unit = (values - center) * inverse
    return (unit, inverse, (unit * norm_gain).astype(jnp.bfloat16))

def norm_back(grad_normed, unit, inverse, norm_gain):
    gscaled = grad_normed.astype(jnp.float32) * norm_gain
    first = lax.optimization_barrier(jnp.mean(gscaled, axis=-1, keepdims=True))
    second = lax.optimization_barrier(jnp.mean(gscaled * unit, axis=-1, keepdims=True))
    return inverse * (gscaled - first - unit * second)

def project(source, qkv_weight):
    flat = source.reshape(-1, source.shape[-1])
    return tuple((jnp.dot(flat, qkv_weight[index], preferred_element_type=jnp.float32).astype(jnp.bfloat16).reshape(source.shape) for index in range(3)))

def project_back(source, grads, qkv_weight):
    flat = source.reshape(-1, source.shape[-1])
    total = jnp.zeros(flat.shape, jnp.float32)
    wgrads = []
    for index in range(3):
        grad_flat = grads[index].reshape(flat.shape)
        total = total + jnp.dot(grad_flat, qkv_weight[index].T, preferred_element_type=jnp.float32)
        wgrads.append(lax.dot_general(flat, grad_flat, (((0,), (0,)), ((), ())), preferred_element_type=jnp.float32))
    return (total.astype(jnp.bfloat16).reshape(source.shape), jnp.stack(wgrads))

def split_heads(values):
    count, pixels, chans = values.shape
    return values.reshape(count, pixels, HEADS, chans // HEADS).astype(jnp.float32)

def attend(queries, keys_all, values_all):
    count, pixels, chans = queries.shape
    factor = (chans // HEADS) ** (-0.5)
    scores = jnp.einsum('fnhd,gnhd->nhfg', split_heads(queries), split_heads(keys_all)) * factor
    probs = jax.nn.softmax(scores, axis=-1)
    weights = probs.astype(jnp.bfloat16).astype(jnp.float32)
    mixed = jnp.einsum('nhfg,gnhd->fnhd', weights, split_heads(values_all))
    return (probs, mixed.reshape(count, pixels, chans).astype(jnp.bfloat16))

def attend_back(probs, queries, keys_all, values_all, grad_mixed):
    count, pixels, chans = queries.shape
    factor = (chans // HEADS) ** (-0.5)
    weights = probs.astype(jnp.bfloat16).astype(jnp.float32)
    grad_heads = split_heads(grad_mixed)
    grad_values = jnp.einsum('nhfg,fnhd->gnhd', weights, grad_heads).astype(jnp.bfloat16)
    grad_probs = jnp.einsum('fnhd,gnhd->nhfg', grad_heads, split_heads(values_all))
    grad_scores = probs * (grad_probs - lax.optimization_barrier(jnp.sum(probs * grad_probs, axis=-1, keepdims=True)))
    grad_scores = (grad_scores * factor).astype(jnp.bfloat16).astype(jnp.float32)
    grad_queries = jnp.einsum('nhfg,gnhd->fnhd', grad_scores, split_heads(keys_all)).astype(jnp.bfloat16)
    grad_keys = jnp.einsum('nhfg,fnhd->gnhd', grad_scores, split_heads(queries)).astype(jnp.bfloat16)
    shape = (count, pixels, chans)
    return (grad_queries.reshape(shape), grad_keys.reshape(shape), grad_values.reshape(shape))

def widen(padded):
    return jnp.pad(padded, ((0, 0), (0, 0), (1, 1), (0, 0)))

def convolve(padded, weight):
    full = widen(padded)
    count, tall, wide, chans = full.shape
    rows, width = (tall - 2, wide - 2)
    total = jnp.zeros((count * rows * width, chans), jnp.float32)
    for row_off in range(3):
        for col_off in range(3):
            slab = full[:, row_off:row_off + rows, col_off:col_off + width].reshape(-1, chans)
            total = total + jnp.dot(slab, weight[row_off, col_off], preferred_element_type=jnp.float32)
    return total.reshape(count, rows, width, chans)

def convolve_back(padded, weight):
    full = widen(padded)
    count, tall, wide, chans = full.shape
    rows, width = (tall - 2, wide - 2)
    total = jnp.zeros((count * rows * width, chans), jnp.float32)
    for row_off in range(3):
        for col_off in range(3):
            slab = full[:, 2 - row_off:2 - row_off + rows, 2 - col_off:2 - col_off + width].reshape(-1, chans)
            total = total + jnp.dot(slab, weight[row_off, col_off].T, preferred_element_type=jnp.float32)
    return total.reshape(count, rows, width, chans)

def kernel_grad(padded, grads):
    full = widen(padded)
    count, tall, wide, chans = full.shape
    rows, width = (tall - 2, wide - 2)
    grad_flat = grads.reshape(-1, chans)
    result = []
    for row_off in range(3):
        for col_off in range(3):
            slab = full[:, row_off:row_off + rows, col_off:col_off + width].reshape(-1, chans)
            result.append(lax.dot_general(slab, grad_flat, (((0,), (0,)), ((), ())), preferred_element_type=jnp.float32))
    return jnp.stack(result).reshape(3, 3, chans, chans)

def reference(frames, norm_gain, qkv_weight, out_weight, conv_weight, out_grad):
    unit, inverse, normed = normalize(frames, norm_gain)
    rows_first = jnp.moveaxis(normed, 1, 0)

    def forward_row(source):
        queries, keys_all, values_all = project(source, qkv_weight)
        return attend(queries, keys_all, values_all)[1]
    mixed = jnp.moveaxis(lax.map(forward_row, rows_first), 0, 1)
    mixed_flat = mixed.reshape(-1, C)
    hidden = frames.astype(jnp.float32) + jnp.dot(mixed_flat, out_weight, preferred_element_type=jnp.float32).reshape(frames.shape)
    act = jax.nn.silu(hidden).astype(jnp.bfloat16)
    act_pad = jnp.pad(act, ((0, 0), (1, 1), (0, 0), (0, 0)))
    output = (hidden + convolve(act_pad, conv_weight)).astype(jnp.bfloat16)
    grad_pad = jnp.pad(out_grad, ((0, 0), (1, 1), (0, 0), (0, 0)))
    grad_act = convolve_back(grad_pad, conv_weight)
    sigma = jax.nn.sigmoid(hidden)
    grad_hidden = out_grad.astype(jnp.float32) + grad_act * sigma * (1.0 + hidden * (1.0 - sigma))
    grad_hidden_b = grad_hidden.astype(jnp.bfloat16).reshape(-1, C)
    grad_out = lax.dot_general(mixed_flat, grad_hidden_b, (((0,), (0,)), ((), ())), preferred_element_type=jnp.float32)
    grad_mixed = jnp.dot(grad_hidden_b, out_weight.T, preferred_element_type=jnp.float32).astype(jnp.bfloat16).reshape(frames.shape)
    grad_conv = kernel_grad(act_pad, out_grad)

    def backward_row(pair):
        source, grad_row = pair
        queries, keys_all, values_all = project(source, qkv_weight)
        probs, unused = attend(queries, keys_all, values_all)
        grads = attend_back(probs, queries, keys_all, values_all, grad_row)
        return project_back(source, grads, qkv_weight)
    grad_rows, qkv_parts = lax.map(backward_row, (rows_first, jnp.moveaxis(grad_mixed, 1, 0)))
    grad_normed = jnp.moveaxis(grad_rows, 0, 1)
    grad_qkv = lax.optimization_barrier(jnp.sum(qkv_parts, axis=0))
    grad_frames = (grad_hidden + norm_back(grad_normed, unit, inverse, norm_gain)).astype(jnp.bfloat16)
    grad_gain = lax.optimization_barrier(jnp.sum((grad_normed.astype(jnp.float32) * unit).reshape(-1, C), axis=0))
    factor = 1.0 / math.sqrt(FRAMES * IMG_H * IMG_W)
    return (output, grad_frames, grad_gain * factor, grad_qkv * factor, grad_out * factor, grad_conv * factor)
```

```python
import math

import jax
import jax.numpy as jnp
from jax import lax
from jax.experimental import pallas as pl
from jax.experimental.pallas import tpu as pltpu
from jax.sharding import PartitionSpec as P

HEADS = 4
EPSILON = 1e-05
MESH = pl.DeviceIdType.MESH
F32 = jnp.float32
BF16 = jnp.bfloat16

NF = 32
NR = 8
C = 128
D = C // HEADS
ROWS = 4
W = 384
PIX = ROWS * W
NC = 3
CP = PIX // NC
M = CP // NF
NG = M // 8
G = 8 * NF

EP = 160
LP = 64
EB = EP // 16
LB = LP // 16


def nn(a, b):
    return jnp.dot(a, b, preferred_element_type=F32)


def nt(a, b):
    return lax.dot_general(a, b, (((1,), (1,)), ((), ())), preferred_element_type=F32)


def tn(a, b):
    return lax.dot_general(a, b, (((0,), (0,)), ((), ())), preferred_element_type=F32)


def rows_of(start, size):
    return pl.ds(pl.multiple_of(start, size), size)


def normalize(values):
    center = jnp.mean(values, axis=-1, keepdims=True)
    spread = jnp.mean(jnp.square(values - center), axis=-1, keepdims=True)
    inverse = lax.rsqrt(spread + EPSILON)
    return (values - center) * inverse, inverse


def kernel(
    factor,
    x_ref, gain_ref, wqkv_ref, wout_ref, wconv_ref, og_ref,
    out_ref, gf_ref, ggain_ref, gqkv_ref, gout_ref, gconv_ref,
    xt, unit_t, stage, k_t, v_s, q_s, n_s, probs,
    mix_s, mix_f, gm_s, gm_t, gn_s, gn_f,
    ogp, actp, gact, hid, gh, act_t, og_sh,
    acc_qkv, acc_gain, acc_out, acc_conv,
    e_s, e_r, e_b, e_br, e_g, e_f,
    l_s, l_r, l_b, l_br, l_g, l_f,
    snd, rcv, hsnd, hrcv, wsnd, wrcv,
):
    f = lax.axis_index("frame")
    r = lax.axis_index("row")
    core = lax.rem(f, 2)
    fx = f // 2
    y = r // 2
    zh = lax.rem(r, 2)
    a = y * 2 + core
    q = zh * 16 + fx

    def frame_peer(k):
        return lax.rem(f + k, NF)

    def a_peer(k):
        a2 = lax.rem(a + k, 8)
        return a2, (fx * 2 + lax.rem(a2, 2), (a2 // 2) * 2 + zh)

    def q_device(q2):
        return (lax.rem(q2, 16) * 2 + core, y * 2 + q2 // 16)

    barrier = pltpu.get_barrier_semaphore()

    @pl.loop(1, NF)
    def _(k):
        pl.semaphore_signal(barrier, inc=1, device_id=(frame_peer(k), r), device_id_type=MESH)
        pl.semaphore_signal(barrier, inc=1, device_id=q_device(lax.rem(q + k, 32)), device_id_type=MESH)

    @pl.loop(1, 8)
    def _(k):
        pl.semaphore_signal(barrier, inc=1, device_id=a_peer(k)[1], device_id_type=MESH)

    @pl.when(r > 0)
    def _():
        pl.semaphore_signal(barrier, inc=1, device_id=(f, r - 1), device_id_type=MESH)

    @pl.when(r < NR - 1)
    def _():
        pl.semaphore_signal(barrier, inc=1, device_id=(f, r + 1), device_id_type=MESH)

    pl.semaphore_wait(barrier, 31 + 31 + 7 + jnp.where(r > 0, 1, 0) + jnp.where(r < NR - 1, 1, 0))

    def to_time(phase, c, src, dst):
        @pl.loop(1, NF)
        def _(k):
            d = frame_peer(k)
            pltpu.make_async_remote_copy(
                src.at[rows_of(c * CP + d * M, M)], dst.at[rows_of(c * CP + f * M, M)],
                snd.at[phase, c], rcv.at[phase, c], device_id=(d, r), device_id_type=MESH,
            ).start()

        own = rows_of(c * CP + f * M, M)
        dst[own, :] = src[own, :]

    def arrived(phase, c, dst):
        view = dst.at[pl.ds(pl.multiple_of(c * CP, M), (NF - 1) * M)]
        pltpu.make_async_copy(view, view, rcv.at[phase, c]).wait()

    def left(phase, c, src):
        view = src.at[pl.ds(pl.multiple_of(c * CP, M), (NF - 1) * M)]
        pltpu.make_async_copy(view, view, snd.at[phase, c]).wait()

    @pl.loop(0, NC)
    def _(c):
        to_time(0, c, x_ref, xt)

    def halo_up(src, dst, s):
        return pltpu.make_async_remote_copy(
            src.at[pl.ds(W, W)], dst.at[pl.ds(5 * W, W)], hsnd.at[s], hrcv.at[s],
            device_id=(f, r - 1), device_id_type=MESH)

    def halo_down(src, dst, s):
        return pltpu.make_async_remote_copy(
            src.at[pl.ds(4 * W, W)], dst.at[pl.ds(0, W)], hsnd.at[s], hrcv.at[s],
            device_id=(f, r + 1), device_id_type=MESH)

    ogp[pl.ds(W, PIX), :] = og_ref[...]

    @pl.when(r > 0)
    def _():
        halo_up(ogp, ogp, 0).start()

    @pl.when(r < NR - 1)
    def _():
        halo_down(ogp, ogp, 1).start()

    edge = jnp.zeros((W, C), BF16)

    @pl.when(r == 0)
    def _():
        ogp[pl.ds(0, W), :] = edge
        actp[pl.ds(0, W), :] = edge

    @pl.when(r == NR - 1)
    def _():
        ogp[pl.ds(5 * W, W), :] = edge
        actp[pl.ds(5 * W, W), :] = edge

    def halo_wait(src, dst, s):
        @pl.when(r > 0)
        def _():
            halo_up(src, dst, s).wait_send()
            halo_down(src, dst, s + 1).wait_recv()

        @pl.when(r < NR - 1)
        def _():
            halo_down(src, dst, s + 1).wait_send()
            halo_up(src, dst, s).wait_recv()

    gain = gain_ref[...]
    wcat = jnp.concatenate([wqkv_ref[0], wqkv_ref[1], wqkv_ref[2]], axis=1)
    scale = D ** (-0.5)
    sub = lax.broadcasted_iota(jnp.int32, (8, G), 0)
    lane = lax.broadcasted_iota(jnp.int32, (8, G), 1)
    diag = (sub == lax.rem(lane, 8)).astype(F32)
    chan = lax.broadcasted_iota(jnp.int32, (1, C), 1) // D
    head_of = [(chan == h).astype(BF16) for h in range(HEADS)]

    acc_qkv[...] = jnp.zeros_like(acc_qkv)
    acc_gain[...] = jnp.zeros_like(acc_gain)
    acc_out[...] = jnp.zeros_like(acc_out)
    acc_conv[...] = jnp.zeros_like(acc_conv)

    @pl.loop(0, NC)
    def _(c):
        arrived(0, c, xt)
        chunk = rows_of(c * CP, CP)
        unit, _ = normalize(xt[chunk, :].astype(F32))
        unit_t[chunk, :] = unit
        stage[...] = (unit * gain).reshape(NF, M, C)

        @pl.loop(0, NG)
        def _(j):
            g = c * NG + j
            eight = pl.ds(pl.multiple_of(j * 8, 8), 8)
            normed = stage[:, eight, :].reshape(G, C).astype(BF16)
            n_s[g] = normed
            qkv = nn(normed, wcat).astype(BF16)
            queries, keys, values = qkv[:, :C], qkv[:, C : 2 * C], qkv[:, 2 * C :]
            q_s[g] = queries
            v_s[g] = values
            q_tr = jnp.transpose(queries)
            k_tr = jnp.transpose(keys)
            v_tr = jnp.transpose(values)
            k_t[g] = k_tr
            parts = []
            for h in range(HEADS):
                s = nn(keys * head_of[h], q_tr).reshape(NF, 8, G)
                top = jnp.max(s, axis=0)
                e = jnp.exp((s - top[None]) * scale)
                inv = diag / jnp.sum(e, axis=0)
                p = (e * inv[None]).reshape(G, G)
                probs[g * HEADS + h] = p
                parts.append(nn(v_tr[h * D : (h + 1) * D], p.astype(BF16)))
            mixed = jnp.transpose(jnp.concatenate(parts, axis=0))
            stage[:, eight, :] = mixed.reshape(NF, 8, C)

        mix_s[chunk, :] = stage[...].reshape(CP, C).astype(BF16)
        to_time(1, c, mix_s, mix_f)

    halo_wait(ogp, ogp, 0)
    col = lax.broadcasted_iota(jnp.int32, (W, C), 0)
    first_col = col == 0
    last_col = col == W - 1

    def after(z):
        return jnp.where(last_col, 0.0, pltpu.roll(z, W - 1, 0))

    def before(z):
        return jnp.where(first_col, 0.0, pltpu.roll(z, 1, 0))

    @pl.loop(0, ROWS)
    def _(row):
        total = jnp.zeros((W, 3 * C), F32)
        for i in range(3):
            total = total + nt(ogp[rows_of((row + 2 - i) * W, W), :], wconv_ref[i])
        here = rows_of(row * W, W)
        gact[here, :] = after(total[:, :C]) + total[:, C : 2 * C] + before(total[:, 2 * C :])
        own = og_ref[here, :].astype(F32)
        og_sh[here, :] = jnp.concatenate(
            [after(own).astype(BF16), og_ref[here, :], before(own).astype(BF16)], axis=1)

    @pl.loop(0, NC)
    def _(c):
        arrived(1, c, mix_f)
        chunk = rows_of(c * CP, CP)
        mixed = mix_f[chunk, :]
        hidden = x_ref[chunk, :].astype(F32) + nn(mixed, wout_ref[...])
        sigma = 1.0 / (1.0 + jnp.exp(-hidden))
        hid[chunk, :] = hidden
        actp[pl.ds(pl.multiple_of(W + c * CP, 128), CP), :] = (hidden * sigma).astype(BF16)
        ghidden = og_ref[chunk, :].astype(F32) + gact[chunk, :] * sigma * (1.0 + hidden * (1.0 - sigma))
        gh[chunk, :] = ghidden
        ghb = ghidden.astype(BF16)
        gm_s[chunk, :] = nt(ghb, wout_ref[...]).astype(BF16)
        to_time(2, c, gm_s, gm_t)
        acc_out[...] += tn(mixed, ghb)

    @pl.when(r > 0)
    def _():
        halo_up(actp, actp, 2).start()

    @pl.when(r < NR - 1)
    def _():
        halo_down(actp, actp, 3).start()

    def sum_a_send(s, size, src, dst):
        @pl.loop(1, 8)
        def _(k):
            a2, dev = a_peer(k)
            pltpu.make_async_remote_copy(
                src.at[rows_of(a2 * size, size)], dst.at[rows_of(a * size, size)],
                wsnd.at[s], wrcv.at[s], device_id=dev, device_id_type=MESH).start()

        own = rows_of(a * size, size)
        dst[own, :] = src[own, :]

    def sum_b_send(s, size, base, src, mid, dst):
        view = src.at[pl.ds(0, 7 * size)]
        pltpu.make_async_copy(view, view, wrcv.at[s - 1]).wait()
        total = src[pl.ds(0, size), :].astype(F32)
        for k in range(1, 8):
            total = total + src[pl.ds(k * size, size), :].astype(F32)
        mid[...] = total.astype(BF16)

        @pl.loop(0, size // 16)
        def _(o):
            owner = base + o

            @pl.when(owner != q)
            def _():
                pltpu.make_async_remote_copy(
                    mid.at[rows_of(o * 16, 16)], dst.at[rows_of(q * 16, 16)],
                    wsnd.at[s], wrcv.at[s], device_id=q_device(owner), device_id_type=MESH).start()

            @pl.when(owner == q)
            def _():
                dst[rows_of(q * 16, 16), :] = mid[rows_of(o * 16, 16), :]

    def owns(size, base):
        return jnp.logical_and(q >= base, q < base + size // 16)

    def sum_b_back(s, size, base, src, dst):
        @pl.when(owns(size, base))
        def _():
            view = src.at[pl.ds(0, 31 * 16)]
            pltpu.make_async_copy(view, view, wrcv.at[s - 1]).wait()
            total = jnp.sum(src[...].astype(F32).reshape(32, 16, C), axis=0) * factor
            mine = rows_of((q - base) * 16, 16)
            dst[mine, :] = total.astype(BF16)

            @pl.loop(1, 32)
            def _(k):
                pltpu.make_async_remote_copy(
                    dst.at[mine], dst.at[mine], wsnd.at[s], wrcv.at[s],
                    device_id=q_device(lax.rem(q + k, 32)), device_id_type=MESH).start()

    def sum_a_back(s, size, base, src, dst):
        nblock = size // 16

        @pl.when(owns(size, base))
        def _():
            view = src.at[pl.ds(0, (nblock - 1) * 16)]
            pltpu.make_async_copy(view, view, wrcv.at[s - 1]).wait()

        @pl.when(jnp.logical_not(owns(size, base)))
        def _():
            view = src.at[pl.ds(0, nblock * 16)]
            pltpu.make_async_copy(view, view, wrcv.at[s - 1]).wait()

        own = rows_of(a * size, size)

        @pl.loop(1, 8)
        def _(k):
            pltpu.make_async_remote_copy(
                src, dst.at[own], wsnd.at[s], wrcv.at[s], device_id=a_peer(k)[1], device_id_type=MESH).start()

        dst[own, :] = src[...]

    def sum_finish(s, size, base, src, mid, back, dst):
        view = dst.at[pl.ds(0, 7 * size)]
        pltpu.make_async_copy(view, view, wrcv.at[s + 3]).wait()
        sent = src.at[pl.ds(0, 7 * size)]
        pltpu.make_async_copy(sent, sent, wsnd.at[s]).wait()
        nblock = size // 16

        @pl.when(owns(size, base))
        def _():
            few = mid.at[pl.ds(0, (nblock - 1) * 16)]
            pltpu.make_async_copy(few, few, wsnd.at[s + 1]).wait()
            many = back.at[pl.ds(0, 31 * 16)]
            pltpu.make_async_copy(many, many, wsnd.at[s + 2]).wait()

        @pl.when(jnp.logical_not(owns(size, base)))
        def _():
            few = mid.at[pl.ds(0, nblock * 16)]
            pltpu.make_async_copy(few, few, wsnd.at[s + 1]).wait()

        pltpu.make_async_copy(view, view, wsnd.at[s + 3]).wait()

    def conv_grad():
        halo_wait(actp, actp, 2)

        @pl.loop(0, ROWS + 2)
        def _(row):
            act_t[row] = jnp.transpose(actp[rows_of(row * W, W), :])

        @pl.loop(0, ROWS)
        def _(row):
            shifted = og_sh[rows_of(row * W, W), :]
            for i in range(3):
                acc_conv[i] += nn(act_t[row + i], shifted)

        for i in range(3):
            for j in range(3):
                at = (3 * i + j) * C
                e_s[at : at + C, :] = acc_conv[i, :, j * C : (j + 1) * C].astype(BF16)
        e_s[9 * C : 10 * C, :] = acc_out[...].astype(BF16)
        sum_a_send(0, EP, e_s, e_r)

    def conv_out():
        @pl.loop(0, ROWS)
        def _(row):
            total = jnp.zeros((W, 3 * C), F32)
            for i in range(3):
                wide = jnp.concatenate([wconv_ref[i, j * C : (j + 1) * C, :] for j in range(3)], axis=1)
                total = total + nn(actp[rows_of((row + i) * W, W), :], wide)
            here = rows_of(row * W, W)
            conv = before(total[:, :C]) + total[:, C : 2 * C] + after(total[:, 2 * C :])
            out_ref[here, :] = (hid[here, :] + conv).astype(BF16)

    @pl.loop(0, NC)
    def _(c):
        arrived(2, c, gm_t)
        chunk = rows_of(c * CP, CP)
        stage[...] = gm_t[chunk, :].astype(F32).reshape(NF, M, C)

        @pl.loop(0, NG)
        def _(j):
            g = c * NG + j
            eight = pl.ds(pl.multiple_of(j * 8, 8), 8)
            gmixed = stage[:, eight, :].reshape(G, C).astype(BF16)
            gm_tr = jnp.transpose(gmixed)
            queries, values, k_tr = q_s[g], v_s[g], k_t[g]
            gk = jnp.zeros((G, C), F32)
            gv = jnp.zeros((G, C), F32)
            parts = []
            for h in range(HEADS):
                gp = nn(values * head_of[h], gm_tr).reshape(NF, 8, G)
                p = probs[g * HEADS + h]
                p3 = p.reshape(NF, 8, G)
                dot = jnp.sum(p3 * gp, axis=0)
                gs = (p3 * (gp - dot[None]) * scale).reshape(G, G).astype(BF16)
                parts.append(nn(k_tr[h * D : (h + 1) * D], gs))
                gk = gk + nn(gs, queries * head_of[h])
                gv = gv + nn(p.astype(BF16), gmixed * head_of[h])
            gq = jnp.transpose(jnp.concatenate(parts, axis=0))
            grads = jnp.concatenate([gq.astype(BF16), gk.astype(BF16), gv.astype(BF16)], axis=1)
            stage[:, eight, :] = nt(grads, wcat).reshape(NF, 8, C)
            acc_qkv[...] += tn(n_s[g], grads)

        gnormed = stage[...].reshape(CP, C).astype(BF16)
        gn_s[chunk, :] = gnormed
        to_time(3, c, gn_s, gn_f)
        acc_gain[...] += jnp.sum((gnormed.astype(F32) * unit_t[chunk, :]).reshape(CP // 8, 8, C), axis=0)

        @pl.when(c == 0)
        def _():
            conv_grad()

        @pl.when(c == 1)
        def _():
            sum_b_send(1, EP, 0, e_r, e_b, e_br)

    for i in range(3):
        for k in range(8):
            lo = max(i * C, k * 48)
            hi = min((i + 1) * C, (k + 1) * 48)
            if lo < hi:
                at = k * LP + lo - k * 48
                l_s[at : at + hi - lo, :] = acc_qkv[lo - i * C : hi - i * C, i * C : (i + 1) * C].astype(BF16)
    total_gain = jnp.sum(acc_gain[...], axis=0, keepdims=True)
    for k in range(8):
        l_s[k * LP + 48 : (k + 1) * LP, :] = jnp.broadcast_to(total_gain, (16, C)).astype(BF16)
    sum_a_send(4, LP, l_s, l_r)
    sum_b_back(2, EP, 0, e_br, e_g)
    conv_out()
    sum_b_send(5, LP, EB, l_r, l_b, l_br)
    sum_a_back(3, EP, 0, e_g, e_f)
    sum_b_back(6, LP, EB, l_br, l_g)

    @pl.loop(0, NC)
    def _(c):
        arrived(3, c, gn_f)
        chunk = rows_of(c * CP, CP)
        unit, inverse = normalize(x_ref[chunk, :].astype(F32))
        gscaled = gn_f[chunk, :].astype(F32) * gain
        first = jnp.mean(gscaled, axis=-1, keepdims=True)
        second = jnp.mean(gscaled * unit, axis=-1, keepdims=True)
        gf_ref[chunk, :] = (gh[chunk, :] + inverse * (gscaled - first - unit * second)).astype(BF16)

    sum_a_back(7, LP, EB, l_g, l_f)
    sum_finish(0, EP, 0, e_r, e_b, e_br, e_f)
    gconv_ref[...] = e_f[: 9 * C, :].astype(F32)
    gout_ref[...] = e_f[9 * C :, :].astype(F32)

    @pl.loop(0, NC)
    def _(c):
        left(0, c, x_ref)
        left(1, c, mix_s)
        left(2, c, gm_s)
        left(3, c, gn_s)

    sum_finish(4, LP, EB, l_r, l_b, l_br, l_f)
    for k in range(8):
        gqkv_ref[k * 48 : (k + 1) * 48, :] = l_f[k * LP : k * LP + 48, :].astype(F32)
    ggain_ref[...] = l_f[48:64, :].astype(F32)[:8]


def on_device(frames, norm_gain, qkv_weight, out_weight, conv_weight, out_grad):
    total_pixels = PIX * NF * NR
    factor = 1.0 / math.sqrt(total_pixels)
    vmem = pl.BlockSpec(memory_space=pltpu.VMEM)
    sds = jax.ShapeDtypeStruct
    full = (PIX, C)
    outs = pl.pallas_call(
        lambda *refs: kernel(factor, *refs),
        out_shape=(
            sds(full, BF16), sds(full, BF16), sds((8, C), F32),
            sds((3 * C, C), F32), sds((C, C), F32), sds((9 * C, C), F32),
        ),
        in_specs=[vmem] * 6,
        out_specs=(vmem,) * 6,
        scratch_shapes=[
            pltpu.VMEM(full, BF16),
            pltpu.VMEM(full, F32),
            pltpu.VMEM((NF, M, C), F32),
            pltpu.VMEM((NC * NG, C, G), BF16),
            pltpu.VMEM((NC * NG, G, C), BF16),
            pltpu.VMEM((NC * NG, G, C), BF16),
            pltpu.VMEM((NC * NG, G, C), BF16),
            pltpu.VMEM((NC * NG * HEADS, G, G), F32),
            pltpu.VMEM(full, BF16),
            pltpu.VMEM(full, BF16),
            pltpu.VMEM(full, BF16),
            pltpu.VMEM(full, BF16),
            pltpu.VMEM(full, BF16),
            pltpu.VMEM(full, BF16),
            pltpu.VMEM((PIX + 2 * W, C), BF16),
            pltpu.VMEM((PIX + 2 * W, C), BF16),
            pltpu.VMEM(full, F32),
            pltpu.VMEM(full, F32),
            pltpu.VMEM(full, F32),
            pltpu.VMEM((ROWS + 2, C, W), BF16),
            pltpu.VMEM((PIX, 3 * C), BF16),
            pltpu.VMEM((C, 3 * C), F32),
            pltpu.VMEM((8, C), F32),
            pltpu.VMEM((C, C), F32),
            pltpu.VMEM((3, C, 3 * C), F32),
            pltpu.VMEM((8 * EP, C), BF16),
            pltpu.VMEM((8 * EP, C), BF16),
            pltpu.VMEM((EP, C), BF16),
            pltpu.VMEM((32 * 16, C), BF16),
            pltpu.VMEM((EP, C), BF16),
            pltpu.VMEM((8 * EP, C), BF16),
            pltpu.VMEM((8 * LP, C), BF16),
            pltpu.VMEM((8 * LP, C), BF16),
            pltpu.VMEM((LP, C), BF16),
            pltpu.VMEM((32 * 16, C), BF16),
            pltpu.VMEM((LP, C), BF16),
            pltpu.VMEM((8 * LP, C), BF16),
            pltpu.SemaphoreType.DMA((4, NC)),
            pltpu.SemaphoreType.DMA((4, NC)),
            pltpu.SemaphoreType.DMA((4,)),
            pltpu.SemaphoreType.DMA((4,)),
            pltpu.SemaphoreType.DMA((8,)),
            pltpu.SemaphoreType.DMA((8,)),
        ],
        compiler_params=pltpu.CompilerParams(
            collective_id=0, has_side_effects=True, vmem_limit_bytes=48 << 20
        ),
        name="block",
    )(
        frames.reshape(full),
        norm_gain.reshape(1, C),
        qkv_weight,
        out_weight,
        conv_weight.reshape(3, 3 * C, C),
        out_grad.reshape(full),
    )
    output, grad_frames, grad_gain, grad_qkv, grad_out, grad_conv = outs
    return (
        output.reshape(frames.shape),
        grad_frames.reshape(frames.shape),
        grad_gain[0],
        grad_qkv.reshape(3, C, C),
        grad_out,
        grad_conv.reshape(3, 3, C, C),
    )


def solution(mesh):
    return jax.shard_map(
        on_device,
        mesh=mesh,
        in_specs=(P("frame", "row", None, None), P(), P(), P(), P(), P("frame", "row", None, None)),
        out_specs=(
            P("frame", "row", None, None),
            P("frame", "row", None, None),
            P(),
            P(),
            P(),
            P(),
        ),
        check_vma=False,
    )
```

```python
import math

import jax
import jax.numpy as jnp
from jax import lax
from jax.experimental import pallas as pl
from jax.experimental.pallas import tpu as pltpu
from jax.sharding import PartitionSpec as P

HEADS = 4
EPSILON = 1e-05
MESH = pl.DeviceIdType.MESH
F32 = jnp.float32
BF16 = jnp.bfloat16

NF = 32
NR = 8
C = 128
D = C // HEADS
ROWS = 4
W = 384
PIX = ROWS * W
NC = 3
CP = PIX // NC
M = CP // NF
NG = M // 8
G = 8 * NF
Q = G // 2
LOG2E = math.log2(math.e)

EP = 160
LP = 64
EB = EP // 16
ACT_PIECES = ((0,), (1,), (2,))
OG_PIECES = ((0, 1, 2), (), ())


def nn(a, b):
    return jnp.dot(a, b, preferred_element_type=F32)


def nt(a, b):
    return lax.dot_general(a, b, (((1,), (1,)), ((), ())), preferred_element_type=F32)


def tn(a, b):
    return lax.dot_general(a, b, (((0,), (0,)), ((), ())), preferred_element_type=F32)


def rows_of(start, size):
    return pl.ds(pl.multiple_of(start, size), size)


def normalize(values):
    center = jnp.mean(values, axis=-1, keepdims=True)
    spread = jnp.mean(jnp.square(values - center), axis=-1, keepdims=True)
    inverse = lax.rsqrt(spread + EPSILON)
    return (values - center) * inverse, inverse


def kernel(
    factor,
    x_hbm, gain_hbm, wqkv_hbm, wout_hbm, wconv_hbm, og_hbm,
    out_hbm, gf_hbm, e_f, l_f,
    x_ref, gain_ref, wqkv_ref, wout_ref, wconv_ref,
    xt, unit_t, stage, k_t, v_s, q_s, n_s, probs,
    mix_s, mix_f, gm_s, gm_t, gn_s, gn_f, out_ref, gf_ref,
    ogp, actp, gact, hid, gh, act_t, og_sh,
    acc_qkv, acc_gain, acc_out,
    e_s, e_r, e_b, e_br, e_g,
    l_s, l_r, l_b, l_br, l_g,
    isem, osem, snd, rcv, hsnd, hrcv, wsnd, wrcv,
):
    f = lax.axis_index("frame")
    r = lax.axis_index("row")
    core = lax.rem(f, 2)
    fx = f // 2
    y = r // 2
    zh = lax.rem(r, 2)
    a = y * 2 + core
    q = zh * 16 + fx

    def frame_peer(k):
        return lax.rem(f + k, NF)

    def a_peer(k):
        a2 = lax.rem(a + k, 8)
        return a2, (fx * 2 + lax.rem(a2, 2), (a2 // 2) * 2 + zh)

    def q_device(q2):
        return (lax.rem(q2, 16) * 2 + core, y * 2 + q2 // 16)

    barrier = pltpu.get_barrier_semaphore()

    fetches = [
        pltpu.make_async_copy(src, dst, isem.at[k])
        for k, (src, dst) in enumerate([
            (x_hbm, x_ref), (gain_hbm, gain_ref), (wqkv_hbm, wqkv_ref), (wout_hbm, wout_ref),
            (wconv_hbm, wconv_ref), (og_hbm, ogp.at[pl.ds(W, PIX)]),
        ])
    ]
    for fetch in fetches:
        fetch.start()

    @pl.loop(1, NF, unroll=True)
    def _(k):
        pl.semaphore_signal(barrier, inc=1, device_id=(frame_peer(k), r), device_id_type=MESH)

    @pl.loop(0, 16, unroll=True)
    def _(k):
        pl.semaphore_signal(barrier, inc=1, device_id=(k * 2 + core, y * 2 + 1 - zh), device_id_type=MESH)

    @pl.loop(2, 8, unroll=True)
    def _(k):
        a2 = lax.rem(y * 2 + k, 8)
        pl.semaphore_signal(
            barrier, inc=1, device_id=(fx * 2 + lax.rem(a2, 2), (a2 // 2) * 2 + zh), device_id_type=MESH)

    @pl.when(r > 0)
    def _():
        pl.semaphore_signal(barrier, inc=1, device_id=(f, r - 1), device_id_type=MESH)

    @pl.when(r < NR - 1)
    def _():
        pl.semaphore_signal(barrier, inc=1, device_id=(f, r + 1), device_id_type=MESH)

    col = lax.broadcasted_iota(jnp.int32, (W, C), 0)
    first_col = col == 0
    last_col = col == W - 1

    def after(z):
        return jnp.where(last_col, 0.0, pltpu.roll(z, W - 1, 0))

    def before(z):
        return jnp.where(first_col, 0.0, pltpu.roll(z, 1, 0))

    def shift_row(row):
        here = rows_of(row * W, W)
        own = ogp[here, :]
        wide = own.astype(F32)
        og_sh[here, :] = jnp.concatenate([after(wide).astype(BF16), own, before(wide).astype(BF16)], axis=1)

    def grad_act_row(row):
        total = jnp.zeros((W, 3 * C), F32)
        for i in range(3):
            total = total + nt(ogp[rows_of((row + 2 - i) * W, W), :], wconv_ref[i])
        gact[rows_of(row * W, W), :] = (
            after(total[:, :C]) + total[:, C : 2 * C] + before(total[:, 2 * C :]))

    for fetch in fetches:
        fetch.wait()

    @pl.loop(1, ROWS - 1)
    def _(row):
        grad_act_row(row)

    @pl.loop(1, ROWS + 1)
    def _(row):
        shift_row(row)

    pl.semaphore_wait(barrier, 31 + 16 + 6 + jnp.where(r > 0, 1, 0) + jnp.where(r < NR - 1, 1, 0))

    def to_time(phase, c, src, dst):
        @pl.loop(1, NF, unroll=True)
        def _(k):
            d = frame_peer(k)
            pltpu.make_async_remote_copy(
                src.at[rows_of(c * CP + d * M, M)], dst.at[rows_of(c * CP + f * M, M)],
                snd.at[phase, c], rcv.at[phase, c], device_id=(d, r), device_id_type=MESH,
            ).start()

        own = rows_of(c * CP + f * M, M)
        dst[own, :] = src[own, :]

    def arrived(phase, c, dst):
        view = dst.at[pl.ds(pl.multiple_of(c * CP, M), (NF - 1) * M)]
        pltpu.make_async_copy(view, view, rcv.at[phase, c]).wait()

    def left(phase, c, src):
        view = src.at[pl.ds(pl.multiple_of(c * CP, M), (NF - 1) * M)]
        pltpu.make_async_copy(view, view, snd.at[phase, c]).wait()

    def turn(t):
        return lax.rem(NC + 1 - t, NC)

    @pl.loop(0, NC)
    def _(t):
        to_time(0, turn(t), x_ref, xt)

    def halo_up(buf, s, piece):
        return pltpu.make_async_remote_copy(
            buf.at[pl.ds(W + piece * C, C)], buf.at[pl.ds(5 * W + piece * C, C)],
            hsnd.at[s, 0, piece], hrcv.at[s, 0, piece], device_id=(f, r - 1), device_id_type=MESH)

    def halo_down(buf, s, piece):
        return pltpu.make_async_remote_copy(
            buf.at[pl.ds(4 * W + piece * C, C)], buf.at[pl.ds(piece * C, C)],
            hsnd.at[s, 1, piece], hrcv.at[s, 1, piece], device_id=(f, r + 1), device_id_type=MESH)

    def halo_start(buf, s, pieces):
        @pl.when(r > 0)
        def _():
            for piece in pieces:
                halo_up(buf, s, piece).start()

        @pl.when(r < NR - 1)
        def _():
            for piece in pieces:
                halo_down(buf, s, piece).start()

    edge = jnp.zeros((W, C), BF16)

    @pl.when(r == 0)
    def _():
        ogp[pl.ds(0, W), :] = edge
        actp[pl.ds(0, W), :] = edge

    @pl.when(r == NR - 1)
    def _():
        ogp[pl.ds(5 * W, W), :] = edge
        actp[pl.ds(5 * W, W), :] = edge

    def halo_wait(buf, s):
        @pl.when(r > 0)
        def _():
            for piece in range(3):
                halo_up(buf, s, piece).wait_send()
                halo_down(buf, s, piece).wait_recv()

        @pl.when(r < NR - 1)
        def _():
            for piece in range(3):
                halo_down(buf, s, piece).wait_send()
                halo_up(buf, s, piece).wait_recv()

    gain = gain_ref[...]
    wcat = jnp.concatenate([wqkv_ref[0], wqkv_ref[1], wqkv_ref[2]], axis=1)
    scale = D ** (-0.5)
    sub = lax.broadcasted_iota(jnp.int32, (8, 2 * Q), 0)
    lane = lax.broadcasted_iota(jnp.int32, (8, 2 * Q), 1)
    diag = (lax.rem(sub, 4) == lax.rem(lane, 4)).astype(F32)
    first_half = lax.broadcasted_iota(jnp.int32, (NF // 2, 8, C), 1) < 4

    def quads(rows):
        lo, hi = rows[: NF // 2], rows[NF // 2 :]
        one = jnp.where(first_half, lo, pltpu.roll(hi, 4, 1)).reshape(Q, C)
        two = jnp.where(first_half, pltpu.roll(lo, 4, 1), hi).reshape(Q, C)
        return jnp.concatenate([one, two], axis=0).astype(BF16)

    def from_quads(rows):
        one = rows[:Q].reshape(NF // 2, 8, C)
        two = rows[Q:].reshape(NF // 2, 8, C)
        lo = jnp.where(first_half, one, pltpu.roll(two, 4, 1))
        hi = jnp.where(first_half, pltpu.roll(one, 4, 1), two)
        return jnp.concatenate([lo, hi], axis=0)

    def two_heads(tr, pair):
        wide = []
        for h in (2 * pair, 2 * pair + 1):
            pieces = [jnp.zeros((h * D, Q), BF16)] if h else []
            pieces.append(tr[h * D : (h + 1) * D])
            if h < HEADS - 1:
                pieces.append(jnp.zeros((C - (h + 1) * D, Q), BF16))
            wide.append(jnp.concatenate(pieces, axis=0))
        return jnp.concatenate(wide, axis=1)

    def by_head(rows):
        return jnp.concatenate([rows * head_of[h] for h in range(HEADS)], axis=0)

    chan = lax.broadcasted_iota(jnp.int32, (1, C), 1) // D
    head_of = [(chan == h).astype(BF16) for h in range(HEADS)]

    acc_qkv[...] = jnp.zeros_like(acc_qkv)
    acc_gain[...] = jnp.zeros_like(acc_gain)
    acc_out[...] = jnp.zeros_like(acc_out)

    @pl.loop(0, NC)
    def _(t):
        c = turn(t)
        arrived(0, c, xt)

        @pl.when(t == 0)
        def _():
            halo_start(ogp, 0, OG_PIECES[0])

        chunk = rows_of(c * CP, CP)
        unit, _ = normalize(xt[chunk, :].astype(F32))
        unit_t[chunk, :] = unit
        stage[...] = (unit * gain).reshape(NF, M, C)

        @pl.loop(0, NG)
        def _(j):
            g = c * NG + j
            eight = pl.ds(pl.multiple_of(j * 8, 8), 8)
            normed = quads(stage[:, eight, :])
            n_s[g] = normed
            qkv = nn(normed, wcat).astype(BF16)
            queries, keys, values = qkv[:, :C], qkv[:, C : 2 * C], qkv[:, 2 * C :]
            q_s[g] = queries
            v_s[g] = values
            q_tr = jnp.transpose(queries)
            k_tr = jnp.transpose(keys)
            v_tr = jnp.transpose(values)
            k_t[g] = k_tr
            mixed = []
            for b in range(2):
                at = slice(b * Q, (b + 1) * Q)
                parts = []
                for pair in range(HEADS // 2):
                    s = nn(keys[at], two_heads(q_tr[:, at], pair)).reshape(Q // 8, 8, 2 * Q)
                    top = jnp.max(s, axis=0)
                    top = jnp.maximum(top, pltpu.roll(top, 4, 0))
                    e = jnp.exp2((s - top[None]) * (scale * LOG2E))
                    below = jnp.sum(e, axis=0)
                    inv = diag / (below + pltpu.roll(below, 4, 0))
                    p = (e * inv[None]).reshape(Q, 2 * Q)
                    probs[(g * 2 + b) * 2 + pair] = p
                    pb = p.astype(BF16)
                    for k in range(2):
                        h = 2 * pair + k
                        parts.append(nn(v_tr[h * D : (h + 1) * D, at], pb[:, k * Q : (k + 1) * Q]))
                mixed.append(jnp.concatenate(parts, axis=0))
            stage[:, eight, :] = from_quads(jnp.transpose(jnp.concatenate(mixed, axis=1)))

        mix_s[chunk, :] = stage[...].reshape(CP, C).astype(BF16)
        to_time(1, c, mix_s, mix_f)

        for late in (1, 2):
            if OG_PIECES[late]:
                @pl.when(t == late - 1)
                def _(late=late):
                    halo_start(ogp, 0, OG_PIECES[late])

    def middle(c):
        arrived(1, c, mix_f)
        chunk = pl.ds(c * CP, CP)
        mixed = mix_f[chunk, :]
        hidden = x_ref[chunk, :].astype(F32) + nn(mixed, wout_ref[...])
        sigma = 1.0 / (1.0 + jnp.exp(-hidden))
        act = (hidden * sigma).astype(BF16)
        ghidden = (ogp[pl.ds(W + c * CP, CP), :].astype(F32)
                   + gact[chunk, :] * sigma * (1.0 + hidden * (1.0 - sigma)))
        ghb = ghidden.astype(BF16)
        gm_s[chunk, :] = nt(ghb, wout_ref[...]).astype(BF16)
        to_time(2, c, gm_s, gm_t)
        hid[chunk, :] = hidden
        actp[pl.ds(W + c * CP, CP), :] = act
        gh[chunk, :] = ghidden
        acc_out[...] += tn(mixed, ghb)
        act_t[:, c * CP : (c + 1) * CP] = jnp.transpose(act)

    middle(1)
    halo_wait(ogp, 0)

    @pl.loop(0, 2)
    def _(k):
        grad_act_row(k * (ROWS - 1))

    middle(0)
    middle(2)

    def sum_a_send(s, size, src, dst):
        @pl.loop(1, 8)
        def _(k):
            a2, dev = a_peer(k)
            pltpu.make_async_remote_copy(
                src.at[rows_of(a2 * size, size)], dst.at[rows_of(a * size, size)],
                wsnd.at[s], wrcv.at[s], device_id=dev, device_id_type=MESH).start()

        own = rows_of(a * size, size)
        dst[own, :] = src[own, :]

    def sum_b_send(s, size, base, src, mid, dst):
        view = src.at[pl.ds(0, 7 * size)]
        pltpu.make_async_copy(view, view, wrcv.at[s - 1]).wait()
        total = src[pl.ds(0, size), :].astype(F32)
        for k in range(1, 8):
            total = total + src[pl.ds(k * size, size), :].astype(F32)
        mid[...] = total.astype(BF16)

        @pl.loop(0, size // 16)
        def _(o):
            owner = 2 * (base + o)

            @pl.when(owner != q)
            def _():
                pltpu.make_async_remote_copy(
                    mid.at[rows_of(o * 16, 16)], dst.at[rows_of(q * 16, 16)],
                    wsnd.at[s], wrcv.at[s], device_id=q_device(owner), device_id_type=MESH).start()

            @pl.when(owner == q)
            def _():
                dst[rows_of(q * 16, 16), :] = mid[rows_of(o * 16, 16), :]

    def owns(size, base):
        return jnp.logical_and(
            lax.rem(q, 2) == 0, jnp.logical_and(q >= 2 * base, q < 2 * base + size // 8))

    def sum_b_back(s, size, base, src, dst):
        @pl.when(owns(size, base))
        def _():
            view = src.at[pl.ds(0, 31 * 16)]
            pltpu.make_async_copy(view, view, wrcv.at[s - 1]).wait()
            total = jnp.sum(src[...].astype(F32).reshape(32, 16, C), axis=0) * factor
            mine = rows_of((q // 2 - base) * 16, 16)
            dst[mine, :] = total.astype(BF16)

            @pl.loop(1, 32)
            def _(k):
                pltpu.make_async_remote_copy(
                    dst.at[mine], dst.at[mine], wsnd.at[s], wrcv.at[s],
                    device_id=q_device(lax.rem(q + k, 32)), device_id_type=MESH).start()

    def sum_a_back(s, size, base, src, dst):
        nblock = size // 16

        @pl.when(owns(size, base))
        def _():
            view = src.at[pl.ds(0, (nblock - 1) * 16)]
            pltpu.make_async_copy(view, view, wrcv.at[s - 1]).wait()

        @pl.when(jnp.logical_not(owns(size, base)))
        def _():
            view = src.at[pl.ds(0, nblock * 16)]
            pltpu.make_async_copy(view, view, wrcv.at[s - 1]).wait()

        own = rows_of(a * size, size)

        @pl.loop(1, 8)
        def _(k):
            pltpu.make_async_remote_copy(
                src, dst.at[own], wsnd.at[s], wrcv.at[s], device_id=a_peer(k)[1], device_id_type=MESH).start()

        pltpu.make_async_copy(src, dst.at[own], osem.at[s // 4]).start()

    def sum_finish(s, size, base, src, mid, back, total, dst):
        own = rows_of(a * size, size)
        pltpu.make_async_copy(total, dst.at[own], osem.at[s // 4]).wait()
        view = dst.at[pl.ds(0, 7 * size)]
        pltpu.make_async_copy(view, view, wrcv.at[s + 3]).wait()
        sent = src.at[pl.ds(0, 7 * size)]
        pltpu.make_async_copy(sent, sent, wsnd.at[s]).wait()
        nblock = size // 16

        @pl.when(owns(size, base))
        def _():
            few = mid.at[pl.ds(0, (nblock - 1) * 16)]
            pltpu.make_async_copy(few, few, wsnd.at[s + 1]).wait()
            many = back.at[pl.ds(0, 31 * 16)]
            pltpu.make_async_copy(many, many, wsnd.at[s + 2]).wait()

        @pl.when(jnp.logical_not(owns(size, base)))
        def _():
            few = mid.at[pl.ds(0, nblock * 16)]
            pltpu.make_async_copy(few, few, wsnd.at[s + 1]).wait()

        pltpu.make_async_copy(view, view, wsnd.at[s + 3]).wait()

    @pl.loop(0, 2)
    def _(k):
        shift_row(k * (ROWS + 1))

    for i in range(3):
        grad = nn(act_t[...], og_sh[(2 - i) * W : (2 - i) * W + PIX, :])
        for j in range(3):
            at = (3 * i + j) * C
            e_s[at : at + C, :] = grad[:, j * C : (j + 1) * C].astype(BF16)
    e_s[9 * C : 10 * C, :] = acc_out[...].astype(BF16)
    sum_a_send(0, EP, e_s, e_r)

    def conv_row(row):
        total = jnp.zeros((W, 3 * C), F32)
        for i in range(3):
            wide = jnp.concatenate([wconv_ref[i, j * C : (j + 1) * C, :] for j in range(3)], axis=1)
            total = total + nn(actp[rows_of((row + i) * W, W), :], wide)
        here = rows_of(row * W, W)
        conv = before(total[:, :C]) + total[:, C : 2 * C] + after(total[:, 2 * C :])
        out_ref[here, :] = (hid[here, :] + conv).astype(BF16)

    @pl.loop(0, NC)
    def _(t):
        c = turn(t)
        arrived(2, c, gm_t)
        chunk = rows_of(c * CP, CP)
        stage[...] = gm_t[chunk, :].astype(F32).reshape(NF, M, C)

        @pl.loop(0, NG)
        def _(j):
            g = c * NG + j
            eight = pl.ds(pl.multiple_of(j * 8, 8), 8)
            gmixed = quads(stage[:, eight, :])
            gm_tr = jnp.transpose(gmixed)
            queries, values, k_tr = q_s[g], v_s[g], k_t[g]
            gqs, gks, gvs = [], [], []
            for b in range(2):
                at = slice(b * Q, (b + 1) * Q)
                parts, scores, weights = [], [], []
                for pair in range(HEADS // 2):
                    gp = nn(values[at], two_heads(gm_tr[:, at], pair)).reshape(Q // 8, 8, 2 * Q)
                    p = probs[(g * 2 + b) * 2 + pair]
                    p3 = p.reshape(Q // 8, 8, 2 * Q)
                    dot = jnp.sum(p3 * gp, axis=0)
                    dot = dot + pltpu.roll(dot, 4, 0)
                    gs = (p3 * (gp - dot[None]) * scale).reshape(Q, 2 * Q).astype(BF16)
                    for k in range(2):
                        h = 2 * pair + k
                        parts.append(nn(k_tr[h * D : (h + 1) * D, at], gs[:, k * Q : (k + 1) * Q]))
                    scores.append(gs)
                    weights.append(p.astype(BF16))
                gqs.append(jnp.concatenate(parts, axis=0))
                gks.append(nn(jnp.concatenate(scores, axis=1), by_head(queries[at])))
                gvs.append(nn(jnp.concatenate(weights, axis=1), by_head(gmixed[at])))
            gq = jnp.transpose(jnp.concatenate(gqs, axis=1))
            gk, gv = jnp.concatenate(gks, axis=0), jnp.concatenate(gvs, axis=0)
            grads = jnp.concatenate([gq.astype(BF16), gk.astype(BF16), gv.astype(BF16)], axis=1)
            stage[:, eight, :] = from_quads(nt(grads, wcat))
            acc_qkv[...] += tn(n_s[g], grads)

        gnormed = stage[...].reshape(CP, C).astype(BF16)
        gn_s[chunk, :] = gnormed
        to_time(3, c, gn_s, gn_f)
        acc_gain[...] += jnp.sum((gnormed.astype(F32) * unit_t[chunk, :]).reshape(CP // 8, 8, C), axis=0)

        @pl.when(t == 1)
        def _():
            sum_b_send(1, EP, 0, e_r, e_b, e_br)

    for i in range(3):
        for k in range(8):
            lo = max(i * C, k * 48)
            hi = min((i + 1) * C, (k + 1) * 48)
            if lo < hi:
                at = k * LP + lo - k * 48
                l_s[at : at + hi - lo, :] = acc_qkv[lo - i * C : hi - i * C, i * C : (i + 1) * C].astype(BF16)
    total_gain = jnp.sum(acc_gain[...], axis=0, keepdims=True)
    for k in range(8):
        l_s[k * LP + 48 : (k + 1) * LP, :] = jnp.broadcast_to(total_gain, (16, C)).astype(BF16)
    sum_a_send(4, LP, l_s, l_r)
    halo_start(actp, 1, ACT_PIECES[0])
    sum_b_back(2, EP, 0, e_br, e_g)

    def put_out(k, at, size):
        rows = pl.ds(at, size)
        return pltpu.make_async_copy(out_ref.at[rows], out_hbm.at[rows], osem.at[2 + k])

    @pl.loop(1, ROWS - 1)
    def _(row):
        conv_row(row)

    put_out(0, W, 2 * W).start()
    sum_b_send(5, LP, EB, l_r, l_b, l_br)
    halo_start(actp, 1, ACT_PIECES[1])
    sum_a_back(3, EP, 0, e_g, e_f)

    def put_gf(c):
        chunk = rows_of(c * CP, CP)
        return pltpu.make_async_copy(gf_ref.at[chunk], gf_hbm.at[chunk], osem.at[5 + c])

    def grad_frames(c):
        arrived(3, c, gn_f)
        chunk = rows_of(c * CP, CP)
        unit, inverse = normalize(x_ref[chunk, :].astype(F32))
        gscaled = gn_f[chunk, :].astype(F32) * gain
        first = jnp.mean(gscaled, axis=-1, keepdims=True)
        second = jnp.mean(gscaled * unit, axis=-1, keepdims=True)
        gf_ref[chunk, :] = (gh[chunk, :] + inverse * (gscaled - first - unit * second)).astype(BF16)
        put_gf(c).start()

    grad_frames(1)
    grad_frames(0)
    sum_b_back(6, LP, EB, l_br, l_g)
    halo_start(actp, 1, ACT_PIECES[2])
    grad_frames(2)
    sum_a_back(7, LP, EB, l_g, l_f)
    halo_wait(actp, 1)

    @pl.loop(0, 2)
    def _(k):
        conv_row(k * (ROWS - 1))

    put_out(1, 0, W).start()
    put_out(2, 3 * W, W).start()
    sum_finish(0, EP, 0, e_r, e_b, e_br, e_g, e_f)

    @pl.loop(0, NC)
    def _(c):
        left(0, c, x_ref)
        left(1, c, mix_s)
        left(2, c, gm_s)
        left(3, c, gn_s)

    for c in range(NC):
        put_gf(c).wait()
    put_out(0, W, 2 * W).wait()
    put_out(1, 0, W).wait()
    put_out(2, 3 * W, W).wait()
    sum_finish(4, LP, EB, l_r, l_b, l_br, l_g, l_f)


def finish(
    out_s, gf_s, e_h, l_h, out_h, gf_h, gain_h, qkv_h, gout_h, conv_h,
    gain, qkv, gout, conv, e_v, l_v, out_v, gf_v, sem,
):
    def put(k, src, dst):
        copy = pltpu.make_async_copy(src, dst, sem.at[k])
        copy.start()
        return copy

    early, late = put(6, e_h, e_v), put(7, l_h, l_v)
    first, second = put(8, out_s, out_v), put(9, gf_s, gf_v)
    copies = []
    early.wait()
    conv[...] = e_v[: 9 * C, :].astype(F32)
    copies.append(put(2, conv, conv_h))
    gout[...] = e_v[9 * C :, :].astype(F32)
    copies.append(put(3, gout, gout_h))
    first.wait()
    copies.append(put(0, out_v, out_h))
    second.wait()
    copies.append(put(1, gf_v, gf_h))
    late.wait()
    for k in range(8):
        qkv[k * 48 : (k + 1) * 48, :] = l_v[k * LP : k * LP + 48, :].astype(F32)
    copies.append(put(4, qkv, qkv_h))
    gain[...] = l_v[48:64, :].astype(F32)[:1]
    copies.append(put(5, gain, gain_h))
    for copy in copies:
        copy.wait()


def on_device(frames, norm_gain, qkv_weight, out_weight, conv_weight, out_grad):
    total_pixels = PIX * NF * NR
    factor = 1.0 / math.sqrt(total_pixels)
    hbm = pl.BlockSpec(memory_space=pltpu.HBM)
    sds = jax.ShapeDtypeStruct
    full = (PIX, C)
    parts = pl.pallas_call(
        lambda *refs: kernel(factor, *refs),
        out_shape=(sds(full, BF16), sds(full, BF16), sds((8 * EP, C), BF16), sds((8 * LP, C), BF16)),
        in_specs=[hbm] * 6,
        out_specs=(hbm,) * 4,
        scratch_shapes=[
            pltpu.VMEM(full, BF16),
            pltpu.VMEM((1, C), F32),
            pltpu.VMEM((3, C, C), BF16),
            pltpu.VMEM((C, C), BF16),
            pltpu.VMEM((3, 3 * C, C), BF16),
            pltpu.VMEM(full, BF16),
            pltpu.VMEM(full, F32),
            pltpu.VMEM((NF, M, C), F32),
            pltpu.VMEM((NC * NG, C, G), BF16),
            pltpu.VMEM((NC * NG, G, C), BF16),
            pltpu.VMEM((NC * NG, G, C), BF16),
            pltpu.VMEM((NC * NG, G, C), BF16),
            pltpu.VMEM((NC * NG * HEADS, Q, 2 * Q), F32),
            pltpu.VMEM(full, BF16),
            pltpu.VMEM(full, BF16),
            pltpu.VMEM(full, BF16),
            pltpu.VMEM(full, BF16),
            pltpu.VMEM(full, BF16),
            pltpu.VMEM(full, BF16),
            pltpu.VMEM(full, BF16),
            pltpu.VMEM(full, BF16),
            pltpu.VMEM((PIX + 2 * W, C), BF16),
            pltpu.VMEM((PIX + 2 * W, C), BF16),
            pltpu.VMEM(full, F32),
            pltpu.VMEM(full, F32),
            pltpu.VMEM(full, F32),
            pltpu.VMEM((C, PIX), BF16),
            pltpu.VMEM((PIX + 2 * W, 3 * C), BF16),
            pltpu.VMEM((C, 3 * C), F32),
            pltpu.VMEM((8, C), F32),
            pltpu.VMEM((C, C), F32),
            pltpu.VMEM((8 * EP, C), BF16),
            pltpu.VMEM((8 * EP, C), BF16),
            pltpu.VMEM((EP, C), BF16),
            pltpu.VMEM((32 * 16, C), BF16),
            pltpu.VMEM((EP, C), BF16),
            pltpu.VMEM((8 * LP, C), BF16),
            pltpu.VMEM((8 * LP, C), BF16),
            pltpu.VMEM((LP, C), BF16),
            pltpu.VMEM((32 * 16, C), BF16),
            pltpu.VMEM((LP, C), BF16),
            pltpu.SemaphoreType.DMA((6,)),
            pltpu.SemaphoreType.DMA((8,)),
            pltpu.SemaphoreType.DMA((4, NC)),
            pltpu.SemaphoreType.DMA((4, NC)),
            pltpu.SemaphoreType.DMA((2, 2, 3)),
            pltpu.SemaphoreType.DMA((2, 2, 3)),
            pltpu.SemaphoreType.DMA((8,)),
            pltpu.SemaphoreType.DMA((8,)),
        ],
        compiler_params=pltpu.CompilerParams(
            collective_id=0, has_side_effects=True, vmem_limit_bytes=60 << 20
        ),
        name="block",
    )(
        frames.reshape(full),
        norm_gain.reshape(1, C),
        qkv_weight,
        out_weight,
        conv_weight.reshape(3, 3 * C, C),
        out_grad.reshape(full),
    )
    sizes = (sds(full, BF16), sds(full, BF16), sds((1, C), F32),
             sds((3 * C, C), F32), sds((C, C), F32), sds((9 * C, C), F32))
    outs = pl.pallas_call(
        finish,
        out_shape=sizes,
        in_specs=[hbm] * 4,
        out_specs=(hbm,) * 6,
        scratch_shapes=[pltpu.VMEM(s.shape, F32) for s in sizes[2:]] + [
            pltpu.VMEM((8 * EP, C), BF16), pltpu.VMEM((8 * LP, C), BF16),
            pltpu.VMEM(full, BF16), pltpu.VMEM(full, BF16), pltpu.SemaphoreType.DMA((10,))],
        compiler_params=pltpu.CompilerParams(vmem_limit_bytes=60 << 20),
        name="finish",
    )(*parts)
    output, grad_frames, grad_gain, grad_qkv, grad_out, grad_conv = outs
    return (
        output.reshape(frames.shape),
        grad_frames.reshape(frames.shape),
        grad_gain.reshape(C),
        grad_qkv.reshape(3, C, C),
        grad_out,
        grad_conv.reshape(3, 3, C, C),
    )


def solution(mesh):
    return jax.shard_map(
        on_device,
        mesh=mesh,
        in_specs=(P("frame", "row", None, None), P(), P(), P(), P(), P("frame", "row", None, None)),
        out_specs=(
            P("frame", "row", None, None),
            P("frame", "row", None, None),
            P(),
            P(),
            P(),
            P(),
        ),
        check_vma=False,
    )
```

```python
import math

import jax
import jax.numpy as jnp
from jax import lax
from jax.experimental import pallas as pl
from jax.experimental.pallas import tpu as pltpu
from jax.sharding import PartitionSpec as P

HEADS = 4
EPSILON = 1e-05
MESH = pl.DeviceIdType.MESH
F32 = jnp.float32
BF16 = jnp.bfloat16

NF = 32
NR = 8
C = 128
D = C // HEADS
ROWS = 4
W = 384
PIX = ROWS * W
NC = 3
CP = PIX // NC
M = CP // NF
NG = M // 8
G = 8 * NF
Q = G // 2
LOG2E = math.log2(math.e)

EP = 160
LP = 64
EB = EP // 16
ACT_PIECES = ((0, 1), (2,), ())
OG_PIECES = ((0, 1, 2), (), ())


def nn(a, b):
    return jnp.dot(a, b, preferred_element_type=F32)


def nt(a, b):
    return lax.dot_general(a, b, (((1,), (1,)), ((), ())), preferred_element_type=F32)


def tn(a, b):
    return lax.dot_general(a, b, (((0,), (0,)), ((), ())), preferred_element_type=F32)


def rows_of(start, size):
    return pl.ds(pl.multiple_of(start, size), size)


def normalize(values):
    center = jnp.mean(values, axis=-1, keepdims=True)
    spread = jnp.mean(jnp.square(values - center), axis=-1, keepdims=True)
    inverse = lax.rsqrt(spread + EPSILON)
    return (values - center) * inverse, inverse


def kernel(
    factor,
    x_hbm, gain_hbm, wqkv_hbm, wout_hbm, wconv_hbm, og_hbm,
    out_hbm, gf_hbm, e_f, l_f,
    x_ref, gain_ref, wqkv_ref, wout_ref, wconv_ref,
    xt, unit_t, stage, k_t, v_s, q_s, n_s, probs,
    mix_s, mix_f, gm_s, gm_t, gn_s, gn_f, out_ref, gf_ref,
    ogp, actp, gact, hid, gh, act_t, og_sh,
    acc_qkv, acc_gain, acc_out,
    e_s, e_r, e_b, e_br, e_g,
    l_s, l_r, l_b, l_br, l_g,
    isem, osem, snd, rcv, hsnd, hrcv, wsnd, wrcv,
):
    f = lax.axis_index("frame")
    r = lax.axis_index("row")
    core = lax.rem(f, 2)
    fx = f // 2
    y = r // 2
    zh = lax.rem(r, 2)
    a = y * 2 + core
    q = zh * 16 + fx

    def frame_peer(k):
        return lax.rem(f + k, NF)

    def a_peer(k):
        a2 = lax.rem(a + k, 8)
        return a2, (fx * 2 + lax.rem(a2, 2), (a2 // 2) * 2 + zh)

    def q_device(q2):
        return (lax.rem(q2, 16) * 2 + core, y * 2 + q2 // 16)

    barrier = pltpu.get_barrier_semaphore()

    fetches = [
        pltpu.make_async_copy(src, dst, isem.at[k])
        for k, (src, dst) in enumerate([
            (x_hbm, x_ref), (gain_hbm, gain_ref), (wqkv_hbm, wqkv_ref), (wout_hbm, wout_ref),
            (wconv_hbm, wconv_ref), (og_hbm, ogp.at[pl.ds(W, PIX)]),
        ])
    ]
    for fetch in fetches:
        fetch.start()

    @pl.loop(1, NF, unroll=True)
    def _(k):
        pl.semaphore_signal(barrier, inc=1, device_id=(frame_peer(k), r), device_id_type=MESH)

    @pl.loop(0, 16, unroll=True)
    def _(k):
        pl.semaphore_signal(barrier, inc=1, device_id=(k * 2 + core, y * 2 + 1 - zh), device_id_type=MESH)

    @pl.loop(2, 8, unroll=True)
    def _(k):
        a2 = lax.rem(y * 2 + k, 8)
        pl.semaphore_signal(
            barrier, inc=1, device_id=(fx * 2 + lax.rem(a2, 2), (a2 // 2) * 2 + zh), device_id_type=MESH)

    @pl.when(r > 0)
    def _():
        pl.semaphore_signal(barrier, inc=1, device_id=(f, r - 1), device_id_type=MESH)

    @pl.when(r < NR - 1)
    def _():
        pl.semaphore_signal(barrier, inc=1, device_id=(f, r + 1), device_id_type=MESH)

    col = lax.broadcasted_iota(jnp.int32, (W, C), 0)
    first_col = col == 0
    last_col = col == W - 1

    def after(z):
        return jnp.where(last_col, 0.0, pltpu.roll(z, W - 1, 0))

    def before(z):
        return jnp.where(first_col, 0.0, pltpu.roll(z, 1, 0))

    def shift_row(row):
        here = rows_of(row * W, W)
        own = ogp[here, :]
        wide = own.astype(F32)
        og_sh[here, :] = jnp.concatenate([after(wide).astype(BF16), own, before(wide).astype(BF16)], axis=1)

    def grad_act_row(row):
        total = jnp.zeros((W, 3 * C), F32)
        for i in range(3):
            total = total + nt(ogp[rows_of((row + 2 - i) * W, W), :], wconv_ref[i])
        gact[rows_of(row * W, W), :] = (
            after(total[:, :C]) + total[:, C : 2 * C] + before(total[:, 2 * C :]))

    for fetch in fetches:
        fetch.wait()

    @pl.loop(1, ROWS - 1)
    def _(row):
        grad_act_row(row)

    @pl.loop(1, ROWS + 1)
    def _(row):
        shift_row(row)

    pl.semaphore_wait(barrier, 31 + 16 + 6 + jnp.where(r > 0, 1, 0) + jnp.where(r < NR - 1, 1, 0))

    def to_time(phase, c, src, dst):
        @pl.loop(1, NF, unroll=True)
        def _(k):
            d = frame_peer(k)
            pltpu.make_async_remote_copy(
                src.at[rows_of(c * CP + d * M, M)], dst.at[rows_of(c * CP + f * M, M)],
                snd.at[phase, c], rcv.at[phase, c], device_id=(d, r), device_id_type=MESH,
            ).start()

        own = rows_of(c * CP + f * M, M)
        dst[own, :] = src[own, :]

    def arrived(phase, c, dst):
        view = dst.at[pl.ds(pl.multiple_of(c * CP, M), (NF - 1) * M)]
        pltpu.make_async_copy(view, view, rcv.at[phase, c]).wait()

    def left(phase, c, src):
        view = src.at[pl.ds(pl.multiple_of(c * CP, M), (NF - 1) * M)]
        pltpu.make_async_copy(view, view, snd.at[phase, c]).wait()

    def turn(t):
        return lax.rem(NC + 1 - t, NC)

    @pl.loop(0, NC)
    def _(t):
        to_time(0, turn(t), x_ref, xt)

    def halo_up(buf, s, piece):
        return pltpu.make_async_remote_copy(
            buf.at[pl.ds(W + piece * C, C)], buf.at[pl.ds(5 * W + piece * C, C)],
            hsnd.at[s, 0, piece], hrcv.at[s, 0, piece], device_id=(f, r - 1), device_id_type=MESH)

    def halo_down(buf, s, piece):
        return pltpu.make_async_remote_copy(
            buf.at[pl.ds(4 * W + piece * C, C)], buf.at[pl.ds(piece * C, C)],
            hsnd.at[s, 1, piece], hrcv.at[s, 1, piece], device_id=(f, r + 1), device_id_type=MESH)

    def halo_start(buf, s, pieces):
        @pl.when(r > 0)
        def _():
            for piece in pieces:
                halo_up(buf, s, piece).start()

        @pl.when(r < NR - 1)
        def _():
            for piece in pieces:
                halo_down(buf, s, piece).start()

    edge = jnp.zeros((W, C), BF16)

    @pl.when(r == 0)
    def _():
        ogp[pl.ds(0, W), :] = edge
        actp[pl.ds(0, W), :] = edge

    @pl.when(r == NR - 1)
    def _():
        ogp[pl.ds(5 * W, W), :] = edge
        actp[pl.ds(5 * W, W), :] = edge

    def halo_wait(buf, s):
        @pl.when(r > 0)
        def _():
            for piece in range(3):
                halo_up(buf, s, piece).wait_send()
                halo_down(buf, s, piece).wait_recv()

        @pl.when(r < NR - 1)
        def _():
            for piece in range(3):
                halo_down(buf, s, piece).wait_send()
                halo_up(buf, s, piece).wait_recv()

    gain = gain_ref[...]
    wcat = jnp.concatenate([wqkv_ref[0], wqkv_ref[1], wqkv_ref[2]], axis=1)
    scale = D ** (-0.5)
    sub = lax.broadcasted_iota(jnp.int32, (8, 2 * Q), 0)
    lane = lax.broadcasted_iota(jnp.int32, (8, 2 * Q), 1)
    diag = (lax.rem(sub, 4) == lax.rem(lane, 4)).astype(F32)
    first_half = lax.broadcasted_iota(jnp.int32, (NF // 2, 8, C), 1) < 4

    def quads(rows):
        lo, hi = rows[: NF // 2], rows[NF // 2 :]
        one = jnp.where(first_half, lo, pltpu.roll(hi, 4, 1)).reshape(Q, C)
        two = jnp.where(first_half, pltpu.roll(lo, 4, 1), hi).reshape(Q, C)
        return jnp.concatenate([one, two], axis=0).astype(BF16)

    def from_quads(rows):
        one = rows[:Q].reshape(NF // 2, 8, C)
        two = rows[Q:].reshape(NF // 2, 8, C)
        lo = jnp.where(first_half, one, pltpu.roll(two, 4, 1))
        hi = jnp.where(first_half, pltpu.roll(one, 4, 1), two)
        return jnp.concatenate([lo, hi], axis=0)

    def two_heads(tr, pair):
        wide = []
        for h in (2 * pair, 2 * pair + 1):
            pieces = [jnp.zeros((h * D, Q), BF16)] if h else []
            pieces.append(tr[h * D : (h + 1) * D])
            if h < HEADS - 1:
                pieces.append(jnp.zeros((C - (h + 1) * D, Q), BF16))
            wide.append(jnp.concatenate(pieces, axis=0))
        return jnp.concatenate(wide, axis=1)

    def by_head(rows):
        return jnp.concatenate([rows * head_of[h] for h in range(HEADS)], axis=0)

    chan = lax.broadcasted_iota(jnp.int32, (1, C), 1) // D
    head_of = [(chan == h).astype(BF16) for h in range(HEADS)]

    acc_qkv[...] = jnp.zeros_like(acc_qkv)
    acc_gain[...] = jnp.zeros_like(acc_gain)
    acc_out[...] = jnp.zeros_like(acc_out)

    @pl.loop(0, NC)
    def _(t):
        c = turn(t)
        arrived(0, c, xt)

        @pl.when(t == 0)
        def _():
            halo_start(ogp, 0, OG_PIECES[0])

        chunk = rows_of(c * CP, CP)
        unit, _ = normalize(xt[chunk, :].astype(F32))
        unit_t[chunk, :] = unit
        stage[...] = (unit * gain).reshape(NF, M, C)

        @pl.loop(0, NG)
        def _(j):
            g = c * NG + j
            eight = pl.ds(pl.multiple_of(j * 8, 8), 8)
            normed = quads(stage[:, eight, :])
            n_s[g] = normed
            qkv = nn(normed, wcat).astype(BF16)
            queries, keys, values = qkv[:, :C], qkv[:, C : 2 * C], qkv[:, 2 * C :]
            q_s[g] = queries
            v_s[g] = values
            q_tr = jnp.transpose(queries)
            k_tr = jnp.transpose(keys)
            v_tr = jnp.transpose(values)
            k_t[g] = k_tr
            mixed = []
            for b in range(2):
                at = slice(b * Q, (b + 1) * Q)
                parts = []
                for pair in range(HEADS // 2):
                    s = nn(keys[at], two_heads(q_tr[:, at], pair)).reshape(Q // 8, 8, 2 * Q)
                    top = jnp.max(s, axis=0)
                    top = jnp.maximum(top, pltpu.roll(top, 4, 0))
                    e = jnp.exp2((s - top[None]) * (scale * LOG2E))
                    below = jnp.sum(e, axis=0)
                    inv = diag / (below + pltpu.roll(below, 4, 0))
                    p = (e * inv[None]).reshape(Q, 2 * Q)
                    probs[(g * 2 + b) * 2 + pair] = p
                    pb = p.astype(BF16)
                    for k in range(2):
                        h = 2 * pair + k
                        parts.append(nn(v_tr[h * D : (h + 1) * D, at], pb[:, k * Q : (k + 1) * Q]))
                mixed.append(jnp.concatenate(parts, axis=0))
            stage[:, eight, :] = from_quads(jnp.transpose(jnp.concatenate(mixed, axis=1)))

        mix_s[chunk, :] = stage[...].reshape(CP, C).astype(BF16)
        to_time(1, c, mix_s, mix_f)

        for late in (1, 2):
            if OG_PIECES[late]:
                @pl.when(t == late - 1)
                def _(late=late):
                    halo_start(ogp, 0, OG_PIECES[late])

    def middle(c):
        arrived(1, c, mix_f)
        chunk = pl.ds(c * CP, CP)
        mixed = mix_f[chunk, :]
        hidden = x_ref[chunk, :].astype(F32) + nn(mixed, wout_ref[...])
        sigma = 1.0 / (1.0 + jnp.exp(-hidden))
        act = (hidden * sigma).astype(BF16)
        ghidden = (ogp[pl.ds(W + c * CP, CP), :].astype(F32)
                   + gact[chunk, :] * sigma * (1.0 + hidden * (1.0 - sigma)))
        ghb = ghidden.astype(BF16)
        gm_s[chunk, :] = nt(ghb, wout_ref[...]).astype(BF16)
        to_time(2, c, gm_s, gm_t)
        hid[chunk, :] = hidden
        actp[pl.ds(W + c * CP, CP), :] = act
        gh[chunk, :] = ghidden
        acc_out[...] += tn(mixed, ghb)
        act_t[:, c * CP : (c + 1) * CP] = jnp.transpose(act)

    middle(1)
    halo_wait(ogp, 0)

    @pl.loop(0, 2)
    def _(k):
        grad_act_row(k * (ROWS - 1))

    middle(0)
    middle(2)

    def sum_a_send(s, size, src, dst):
        @pl.loop(1, 8)
        def _(k):
            a2, dev = a_peer(k)
            pltpu.make_async_remote_copy(
                src.at[rows_of(a2 * size, size)], dst.at[rows_of(a * size, size)],
                wsnd.at[s], wrcv.at[s], device_id=dev, device_id_type=MESH).start()

        own = rows_of(a * size, size)
        dst[own, :] = src[own, :]

    def sum_b_send(s, size, base, src, mid, dst):
        view = src.at[pl.ds(0, 7 * size)]
        pltpu.make_async_copy(view, view, wrcv.at[s - 1]).wait()
        total = src[pl.ds(0, size), :].astype(F32)
        for k in range(1, 8):
            total = total + src[pl.ds(k * size, size), :].astype(F32)
        mid[...] = total.astype(BF16)

        @pl.loop(0, size // 16)
        def _(o):
            owner = 2 * (base + o)

            @pl.when(owner != q)
            def _():
                pltpu.make_async_remote_copy(
                    mid.at[rows_of(o * 16, 16)], dst.at[rows_of(q * 16, 16)],
                    wsnd.at[s], wrcv.at[s], device_id=q_device(owner), device_id_type=MESH).start()

            @pl.when(owner == q)
            def _():
                dst[rows_of(q * 16, 16), :] = mid[rows_of(o * 16, 16), :]

    def owns(size, base):
        return jnp.logical_and(
            lax.rem(q, 2) == 0, jnp.logical_and(q >= 2 * base, q < 2 * base + size // 8))

    def sum_b_back(s, size, base, src, dst):
        @pl.when(owns(size, base))
        def _():
            view = src.at[pl.ds(0, 31 * 16)]
            pltpu.make_async_copy(view, view, wrcv.at[s - 1]).wait()
            total = jnp.sum(src[...].astype(F32).reshape(32, 16, C), axis=0) * factor
            mine = rows_of((q // 2 - base) * 16, 16)
            dst[mine, :] = total.astype(BF16)

            @pl.loop(1, 32)
            def _(k):
                pltpu.make_async_remote_copy(
                    dst.at[mine], dst.at[mine], wsnd.at[s], wrcv.at[s],
                    device_id=q_device(lax.rem(q + k, 32)), device_id_type=MESH).start()

    def sum_a_back(s, size, base, src, dst):
        nblock = size // 16

        @pl.when(owns(size, base))
        def _():
            view = src.at[pl.ds(0, (nblock - 1) * 16)]
            pltpu.make_async_copy(view, view, wrcv.at[s - 1]).wait()

        @pl.when(jnp.logical_not(owns(size, base)))
        def _():
            view = src.at[pl.ds(0, nblock * 16)]
            pltpu.make_async_copy(view, view, wrcv.at[s - 1]).wait()

        own = rows_of(a * size, size)

        @pl.loop(1, 8)
        def _(k):
            pltpu.make_async_remote_copy(
                src, dst.at[own], wsnd.at[s], wrcv.at[s], device_id=a_peer(k)[1], device_id_type=MESH).start()

        pltpu.make_async_copy(src, dst.at[own], osem.at[s // 4]).start()

    def sum_finish(s, size, base, src, mid, back, total, dst):
        own = rows_of(a * size, size)
        pltpu.make_async_copy(total, dst.at[own], osem.at[s // 4]).wait()
        view = dst.at[pl.ds(0, 7 * size)]
        pltpu.make_async_copy(view, view, wrcv.at[s + 3]).wait()
        sent = src.at[pl.ds(0, 7 * size)]
        pltpu.make_async_copy(sent, sent, wsnd.at[s]).wait()
        nblock = size // 16

        @pl.when(owns(size, base))
        def _():
            few = mid.at[pl.ds(0, (nblock - 1) * 16)]
            pltpu.make_async_copy(few, few, wsnd.at[s + 1]).wait()
            many = back.at[pl.ds(0, 31 * 16)]
            pltpu.make_async_copy(many, many, wsnd.at[s + 2]).wait()

        @pl.when(jnp.logical_not(owns(size, base)))
        def _():
            few = mid.at[pl.ds(0, nblock * 16)]
            pltpu.make_async_copy(few, few, wsnd.at[s + 1]).wait()

        pltpu.make_async_copy(view, view, wsnd.at[s + 3]).wait()

    @pl.loop(0, 2)
    def _(k):
        shift_row(k * (ROWS + 1))

    for i in range(3):
        grad = nn(act_t[...], og_sh[(2 - i) * W : (2 - i) * W + PIX, :])
        for j in range(3):
            at = (3 * i + j) * C
            e_s[at : at + C, :] = grad[:, j * C : (j + 1) * C].astype(BF16)
    e_s[9 * C : 10 * C, :] = acc_out[...].astype(BF16)

    def conv_row(row):
        total = jnp.zeros((W, 3 * C), F32)
        for i in range(3):
            wide = jnp.concatenate([wconv_ref[i, j * C : (j + 1) * C, :] for j in range(3)], axis=1)
            total = total + nn(actp[rows_of((row + i) * W, W), :], wide)
        here = rows_of(row * W, W)
        conv = before(total[:, :C]) + total[:, C : 2 * C] + after(total[:, 2 * C :])
        out_ref[here, :] = (hid[here, :] + conv).astype(BF16)

    @pl.loop(0, NC)
    def _(t):
        c = turn(t)
        arrived(2, c, gm_t)
        chunk = rows_of(c * CP, CP)
        stage[...] = gm_t[chunk, :].astype(F32).reshape(NF, M, C)

        @pl.loop(0, NG)
        def _(j):
            g = c * NG + j
            eight = pl.ds(pl.multiple_of(j * 8, 8), 8)
            gmixed = quads(stage[:, eight, :])
            gm_tr = jnp.transpose(gmixed)
            queries, values, k_tr = q_s[g], v_s[g], k_t[g]
            gqs, gks, gvs = [], [], []
            for b in range(2):
                at = slice(b * Q, (b + 1) * Q)
                parts, scores, weights = [], [], []
                for pair in range(HEADS // 2):
                    gp = nn(values[at], two_heads(gm_tr[:, at], pair)).reshape(Q // 8, 8, 2 * Q)
                    p = probs[(g * 2 + b) * 2 + pair]
                    p3 = p.reshape(Q // 8, 8, 2 * Q)
                    dot = jnp.sum(p3 * gp, axis=0)
                    dot = dot + pltpu.roll(dot, 4, 0)
                    gs = (p3 * (gp - dot[None]) * scale).reshape(Q, 2 * Q).astype(BF16)
                    for k in range(2):
                        h = 2 * pair + k
                        parts.append(nn(k_tr[h * D : (h + 1) * D, at], gs[:, k * Q : (k + 1) * Q]))
                    scores.append(gs)
                    weights.append(p.astype(BF16))
                gqs.append(jnp.concatenate(parts, axis=0))
                gks.append(nn(jnp.concatenate(scores, axis=1), by_head(queries[at])))
                gvs.append(nn(jnp.concatenate(weights, axis=1), by_head(gmixed[at])))
            gq = jnp.transpose(jnp.concatenate(gqs, axis=1))
            gk, gv = jnp.concatenate(gks, axis=0), jnp.concatenate(gvs, axis=0)
            grads = jnp.concatenate([gq.astype(BF16), gk.astype(BF16), gv.astype(BF16)], axis=1)
            stage[:, eight, :] = from_quads(nt(grads, wcat))
            acc_qkv[...] += tn(n_s[g], grads)

        gnormed = stage[...].reshape(CP, C).astype(BF16)
        gn_s[chunk, :] = gnormed
        to_time(3, c, gn_s, gn_f)
        @pl.when(t == 0)
        def _():
            sum_a_send(0, EP, e_s, e_r)

        acc_gain[...] += jnp.sum((gnormed.astype(F32) * unit_t[chunk, :]).reshape(CP // 8, 8, C), axis=0)


    for i in range(3):
        for k in range(8):
            lo = max(i * C, k * 48)
            hi = min((i + 1) * C, (k + 1) * 48)
            if lo < hi:
                at = k * LP + lo - k * 48
                l_s[at : at + hi - lo, :] = acc_qkv[lo - i * C : hi - i * C, i * C : (i + 1) * C].astype(BF16)
    total_gain = jnp.sum(acc_gain[...], axis=0, keepdims=True)
    for k in range(8):
        l_s[k * LP + 48 : (k + 1) * LP, :] = jnp.broadcast_to(total_gain, (16, C)).astype(BF16)
    sum_a_send(4, LP, l_s, l_r)
    halo_start(actp, 1, ACT_PIECES[0])

    def put_out(k, at, size):
        rows = pl.ds(at, size)
        return pltpu.make_async_copy(out_ref.at[rows], out_hbm.at[rows], osem.at[2 + k])

    @pl.loop(1, ROWS - 1)
    def _(row):
        conv_row(row)

    put_out(0, W, 2 * W).start()
    sum_b_send(5, LP, EB, l_r, l_b, l_br)
    sum_b_send(1, EP, 0, e_r, e_b, e_br)
    halo_start(actp, 1, ACT_PIECES[1])

    def put_gf(c):
        chunk = rows_of(c * CP, CP)
        return pltpu.make_async_copy(gf_ref.at[chunk], gf_hbm.at[chunk], osem.at[5 + c])

    def grad_frames(c):
        arrived(3, c, gn_f)
        chunk = rows_of(c * CP, CP)
        unit, inverse = normalize(x_ref[chunk, :].astype(F32))
        gscaled = gn_f[chunk, :].astype(F32) * gain
        first = jnp.mean(gscaled, axis=-1, keepdims=True)
        second = jnp.mean(gscaled * unit, axis=-1, keepdims=True)
        gf_ref[chunk, :] = (gh[chunk, :] + inverse * (gscaled - first - unit * second)).astype(BF16)
        put_gf(c).start()

    grad_frames(1)
    grad_frames(0)
    sum_b_back(6, LP, EB, l_br, l_g)
    sum_b_back(2, EP, 0, e_br, e_g)
    halo_start(actp, 1, ACT_PIECES[2])
    grad_frames(2)
    sum_a_back(7, LP, EB, l_g, l_f)
    sum_a_back(3, EP, 0, e_g, e_f)
    halo_wait(actp, 1)

    @pl.loop(0, 2)
    def _(k):
        conv_row(k * (ROWS - 1))

    put_out(1, 0, W).start()
    put_out(2, 3 * W, W).start()
    sum_finish(0, EP, 0, e_r, e_b, e_br, e_g, e_f)

    @pl.loop(0, NC)
    def _(c):
        left(0, c, x_ref)
        left(1, c, mix_s)
        left(2, c, gm_s)
        left(3, c, gn_s)

    for c in range(NC):
        put_gf(c).wait()
    put_out(0, W, 2 * W).wait()
    put_out(1, 0, W).wait()
    put_out(2, 3 * W, W).wait()
    sum_finish(4, LP, EB, l_r, l_b, l_br, l_g, l_f)


def finish(
    out_s, gf_s, e_h, l_h, out_h, gf_h, gain_h, qkv_h, gout_h, conv_h,
    gain, qkv, gout, conv, e_v, l_v, out_v, gf_v, sem,
):
    def put(k, src, dst):
        copy = pltpu.make_async_copy(src, dst, sem.at[k])
        copy.start()
        return copy

    early, late = put(6, e_h, e_v), put(7, l_h, l_v)
    first, second = put(8, out_s, out_v), put(9, gf_s, gf_v)
    copies = []
    early.wait()
    conv[...] = e_v[: 9 * C, :].astype(F32)
    copies.append(put(2, conv, conv_h))
    gout[...] = e_v[9 * C :, :].astype(F32)
    copies.append(put(3, gout, gout_h))
    first.wait()
    copies.append(put(0, out_v, out_h))
    second.wait()
    copies.append(put(1, gf_v, gf_h))
    late.wait()
    for k in range(8):
        qkv[k * 48 : (k + 1) * 48, :] = l_v[k * LP : k * LP + 48, :].astype(F32)
    copies.append(put(4, qkv, qkv_h))
    gain[...] = l_v[48:64, :].astype(F32)[:1]
    copies.append(put(5, gain, gain_h))
    for copy in copies:
        copy.wait()


def on_device(frames, norm_gain, qkv_weight, out_weight, conv_weight, out_grad):
    total_pixels = PIX * NF * NR
    factor = 1.0 / math.sqrt(total_pixels)
    hbm = pl.BlockSpec(memory_space=pltpu.HBM)
    sds = jax.ShapeDtypeStruct
    full = (PIX, C)
    parts = pl.pallas_call(
        lambda *refs: kernel(factor, *refs),
        out_shape=(sds(full, BF16), sds(full, BF16), sds((8 * EP, C), BF16), sds((8 * LP, C), BF16)),
        in_specs=[hbm] * 6,
        out_specs=(hbm,) * 4,
        scratch_shapes=[
            pltpu.VMEM(full, BF16),
            pltpu.VMEM((1, C), F32),
            pltpu.VMEM((3, C, C), BF16),
            pltpu.VMEM((C, C), BF16),
            pltpu.VMEM((3, 3 * C, C), BF16),
            pltpu.VMEM(full, BF16),
            pltpu.VMEM(full, F32),
            pltpu.VMEM((NF, M, C), F32),
            pltpu.VMEM((NC * NG, C, G), BF16),
            pltpu.VMEM((NC * NG, G, C), BF16),
            pltpu.VMEM((NC * NG, G, C), BF16),
            pltpu.VMEM((NC * NG, G, C), BF16),
            pltpu.VMEM((NC * NG * HEADS, Q, 2 * Q), F32),
            pltpu.VMEM(full, BF16),
            pltpu.VMEM(full, BF16),
            pltpu.VMEM(full, BF16),
            pltpu.VMEM(full, BF16),
            pltpu.VMEM(full, BF16),
            pltpu.VMEM(full, BF16),
            pltpu.VMEM(full, BF16),
            pltpu.VMEM(full, BF16),
            pltpu.VMEM((PIX + 2 * W, C), BF16),
            pltpu.VMEM((PIX + 2 * W, C), BF16),
            pltpu.VMEM(full, F32),
            pltpu.VMEM(full, F32),
            pltpu.VMEM(full, F32),
            pltpu.VMEM((C, PIX), BF16),
            pltpu.VMEM((PIX + 2 * W, 3 * C), BF16),
            pltpu.VMEM((C, 3 * C), F32),
            pltpu.VMEM((8, C), F32),
            pltpu.VMEM((C, C), F32),
            pltpu.VMEM((8 * EP, C), BF16),
            pltpu.VMEM((8 * EP, C), BF16),
            pltpu.VMEM((EP, C), BF16),
            pltpu.VMEM((32 * 16, C), BF16),
            pltpu.VMEM((EP, C), BF16),
            pltpu.VMEM((8 * LP, C), BF16),
            pltpu.VMEM((8 * LP, C), BF16),
            pltpu.VMEM((LP, C), BF16),
            pltpu.VMEM((32 * 16, C), BF16),
            pltpu.VMEM((LP, C), BF16),
            pltpu.SemaphoreType.DMA((6,)),
            pltpu.SemaphoreType.DMA((8,)),
            pltpu.SemaphoreType.DMA((4, NC)),
            pltpu.SemaphoreType.DMA((4, NC)),
            pltpu.SemaphoreType.DMA((2, 2, 3)),
            pltpu.SemaphoreType.DMA((2, 2, 3)),
            pltpu.SemaphoreType.DMA((8,)),
            pltpu.SemaphoreType.DMA((8,)),
        ],
        compiler_params=pltpu.CompilerParams(
            collective_id=0, has_side_effects=True, vmem_limit_bytes=60 << 20
        ),
        name="block",
    )(
        frames.reshape(full),
        norm_gain.reshape(1, C),
        qkv_weight,
        out_weight,
        conv_weight.reshape(3, 3 * C, C),
        out_grad.reshape(full),
    )
    sizes = (sds(full, BF16), sds(full, BF16), sds((1, C), F32),
             sds((3 * C, C), F32), sds((C, C), F32), sds((9 * C, C), F32))
    outs = pl.pallas_call(
        finish,
        out_shape=sizes,
        in_specs=[hbm] * 4,
        out_specs=(hbm,) * 6,
        scratch_shapes=[pltpu.VMEM(s.shape, F32) for s in sizes[2:]] + [
            pltpu.VMEM((8 * EP, C), BF16), pltpu.VMEM((8 * LP, C), BF16),
            pltpu.VMEM(full, BF16), pltpu.VMEM(full, BF16), pltpu.SemaphoreType.DMA((10,))],
        compiler_params=pltpu.CompilerParams(vmem_limit_bytes=60 << 20),
        name="finish",
    )(*parts)
    output, grad_frames, grad_gain, grad_qkv, grad_out, grad_conv = outs
    return (
        output.reshape(frames.shape),
        grad_frames.reshape(frames.shape),
        grad_gain.reshape(C),
        grad_qkv.reshape(3, C, C),
        grad_out,
        grad_conv.reshape(3, 3, C, C),
    )


def solution(mesh):
    return jax.shard_map(
        on_device,
        mesh=mesh,
        in_specs=(P("frame", "row", None, None), P(), P(), P(), P(), P("frame", "row", None, None)),
        out_specs=(
            P("frame", "row", None, None),
            P("frame", "row", None, None),
            P(),
            P(),
            P(),
            P(),
        ),
        check_vma=False,
    )
```

```python
import math

import jax
import jax.numpy as jnp
from jax import lax
from jax.experimental import pallas as pl
from jax.experimental.pallas import tpu as pltpu
from jax.sharding import PartitionSpec as P

HEADS = 4
EPSILON = 1e-05
MESH = pl.DeviceIdType.MESH
F32 = jnp.float32
BF16 = jnp.bfloat16

NF = 32
NR = 8
C = 128
D = C // HEADS
ROWS = 4
W = 384
PIX = ROWS * W
NC = 3
CP = PIX // NC
M = CP // NF
NG = M // 8
G = 8 * NF
Q = G // 2
LOG2E = math.log2(math.e)

EP = 160
LP = 64
EB = EP // 16
ACT_PIECES = ((0, 1), (2,), ())
OG_PIECES = ((), (0, 1, 2), ())


def nn(a, b):
    return jnp.dot(a, b, preferred_element_type=F32)


def nt(a, b):
    return lax.dot_general(a, b, (((1,), (1,)), ((), ())), preferred_element_type=F32)


def tn(a, b):
    return lax.dot_general(a, b, (((0,), (0,)), ((), ())), preferred_element_type=F32)


def rows_of(start, size):
    return pl.ds(pl.multiple_of(start, size), size)


def normalize(values):
    center = jnp.mean(values, axis=-1, keepdims=True)
    spread = jnp.mean(jnp.square(values - center), axis=-1, keepdims=True)
    inverse = lax.rsqrt(spread + EPSILON)
    return (values - center) * inverse, inverse


def kernel(
    factor,
    x_hbm, gain_hbm, wqkv_hbm, wout_hbm, wconv_hbm, og_hbm,
    out_hbm, gf_hbm, e_f, l_f,
    x_ref, gain_ref, wqkv_ref, wout_ref, wconv_ref,
    xt, unit_t, stage, k_t, v_s, q_s, n_s, probs,
    mix_s, mix_f, gm_s, gm_t, gn_s, gn_f, out_ref, gf_ref,
    ogp, actp, gact, hid, gh, act_t, og_sh,
    acc_qkv, acc_gain, acc_out,
    e_s, e_r, e_b, e_br, e_g,
    l_s, l_r, l_b, l_br, l_g,
    isem, osem, snd, rcv, hsnd, hrcv, wsnd, wrcv,
):
    f = lax.axis_index("frame")
    r = lax.axis_index("row")
    core = lax.rem(f, 2)
    fx = f // 2
    y = r // 2
    zh = lax.rem(r, 2)
    a = y * 2 + core
    q = zh * 16 + fx

    def frame_peer(k):
        return lax.rem(f + k, NF)

    def a_peer(k):
        a2 = lax.rem(a + k, 8)
        return a2, (fx * 2 + lax.rem(a2, 2), (a2 // 2) * 2 + zh)

    def q_device(q2):
        return (lax.rem(q2, 16) * 2 + core, y * 2 + q2 // 16)

    barrier = pltpu.get_barrier_semaphore()

    fetches = [
        pltpu.make_async_copy(src, dst, isem.at[k])
        for k, (src, dst) in enumerate([
            (x_hbm, x_ref), (gain_hbm, gain_ref), (wqkv_hbm, wqkv_ref), (wout_hbm, wout_ref),
            (wconv_hbm, wconv_ref), (og_hbm, ogp.at[pl.ds(W, PIX)]),
        ])
    ]
    for fetch in fetches:
        fetch.start()

    @pl.loop(1, NF, unroll=True)
    def _(k):
        pl.semaphore_signal(barrier, inc=1, device_id=(frame_peer(k), r), device_id_type=MESH)

    @pl.loop(0, 16, unroll=True)
    def _(k):
        pl.semaphore_signal(barrier, inc=1, device_id=(k * 2 + core, y * 2 + 1 - zh), device_id_type=MESH)

    @pl.loop(2, 8, unroll=True)
    def _(k):
        a2 = lax.rem(y * 2 + k, 8)
        pl.semaphore_signal(
            barrier, inc=1, device_id=(fx * 2 + lax.rem(a2, 2), (a2 // 2) * 2 + zh), device_id_type=MESH)

    @pl.when(r > 0)
    def _():
        pl.semaphore_signal(barrier, inc=1, device_id=(f, r - 1), device_id_type=MESH)

    @pl.when(r < NR - 1)
    def _():
        pl.semaphore_signal(barrier, inc=1, device_id=(f, r + 1), device_id_type=MESH)

    col = lax.broadcasted_iota(jnp.int32, (W, C), 0)
    first_col = col == 0
    last_col = col == W - 1

    def after(z):
        return jnp.where(last_col, 0.0, pltpu.roll(z, W - 1, 0))

    def before(z):
        return jnp.where(first_col, 0.0, pltpu.roll(z, 1, 0))

    def shift_row(row):
        here = rows_of(row * W, W)
        own = ogp[here, :]
        wide = own.astype(F32)
        og_sh[here, :] = jnp.concatenate([after(wide).astype(BF16), own, before(wide).astype(BF16)], axis=1)

    def grad_act_row(row):
        total = jnp.zeros((W, 3 * C), F32)
        for i in range(3):
            total = total + nt(ogp[rows_of((row + 2 - i) * W, W), :], wconv_ref[i])
        gact[rows_of(row * W, W), :] = (
            after(total[:, :C]) + total[:, C : 2 * C] + before(total[:, 2 * C :]))

    for fetch in fetches:
        fetch.wait()

    @pl.loop(1, ROWS - 1)
    def _(row):
        grad_act_row(row)

    @pl.loop(1, ROWS + 1)
    def _(row):
        shift_row(row)

    pl.semaphore_wait(barrier, 31 + 16 + 6 + jnp.where(r > 0, 1, 0) + jnp.where(r < NR - 1, 1, 0))

    def to_time(phase, c, src, dst):
        @pl.loop(1, NF, unroll=True)
        def _(k):
            d = frame_peer(k)
            pltpu.make_async_remote_copy(
                src.at[rows_of(c * CP + d * M, M)], dst.at[rows_of(c * CP + f * M, M)],
                snd.at[phase, c], rcv.at[phase, c], device_id=(d, r), device_id_type=MESH,
            ).start()

        own = rows_of(c * CP + f * M, M)
        dst[own, :] = src[own, :]

    def arrived(phase, c, dst):
        view = dst.at[pl.ds(pl.multiple_of(c * CP, M), (NF - 1) * M)]
        pltpu.make_async_copy(view, view, rcv.at[phase, c]).wait()

    def left(phase, c, src):
        view = src.at[pl.ds(pl.multiple_of(c * CP, M), (NF - 1) * M)]
        pltpu.make_async_copy(view, view, snd.at[phase, c]).wait()

    def turn(t):
        return lax.rem(NC + 1 - t, NC)

    @pl.loop(0, NC)
    def _(t):
        to_time(0, turn(t), x_ref, xt)

    def halo_up(buf, s, piece):
        return pltpu.make_async_remote_copy(
            buf.at[pl.ds(W + piece * C, C)], buf.at[pl.ds(5 * W + piece * C, C)],
            hsnd.at[s, 0, piece], hrcv.at[s, 0, piece], device_id=(f, r - 1), device_id_type=MESH)

    def halo_down(buf, s, piece):
        return pltpu.make_async_remote_copy(
            buf.at[pl.ds(4 * W + piece * C, C)], buf.at[pl.ds(piece * C, C)],
            hsnd.at[s, 1, piece], hrcv.at[s, 1, piece], device_id=(f, r + 1), device_id_type=MESH)

    def halo_start(buf, s, pieces):
        @pl.when(r > 0)
        def _():
            for piece in pieces:
                halo_up(buf, s, piece).start()

        @pl.when(r < NR - 1)
        def _():
            for piece in pieces:
                halo_down(buf, s, piece).start()

    edge = jnp.zeros((W, C), BF16)

    @pl.when(r == 0)
    def _():
        ogp[pl.ds(0, W), :] = edge
        actp[pl.ds(0, W), :] = edge

    @pl.when(r == NR - 1)
    def _():
        ogp[pl.ds(5 * W, W), :] = edge
        actp[pl.ds(5 * W, W), :] = edge

    def halo_wait(buf, s):
        @pl.when(r > 0)
        def _():
            for piece in range(3):
                halo_up(buf, s, piece).wait_send()
                halo_down(buf, s, piece).wait_recv()

        @pl.when(r < NR - 1)
        def _():
            for piece in range(3):
                halo_down(buf, s, piece).wait_send()
                halo_up(buf, s, piece).wait_recv()

    gain = gain_ref[...]
    wcat = jnp.concatenate([wqkv_ref[0], wqkv_ref[1], wqkv_ref[2]], axis=1)
    scale = D ** (-0.5)
    sub = lax.broadcasted_iota(jnp.int32, (8, 2 * Q), 0)
    lane = lax.broadcasted_iota(jnp.int32, (8, 2 * Q), 1)
    diag = (lax.rem(sub, 4) == lax.rem(lane, 4)).astype(F32)
    first_half = lax.broadcasted_iota(jnp.int32, (NF // 2, 8, C), 1) < 4

    def quads(rows):
        lo, hi = rows[: NF // 2], rows[NF // 2 :]
        one = jnp.where(first_half, lo, pltpu.roll(hi, 4, 1)).reshape(Q, C)
        two = jnp.where(first_half, pltpu.roll(lo, 4, 1), hi).reshape(Q, C)
        return jnp.concatenate([one, two], axis=0).astype(BF16)

    def from_quads(rows):
        one = rows[:Q].reshape(NF // 2, 8, C)
        two = rows[Q:].reshape(NF // 2, 8, C)
        lo = jnp.where(first_half, one, pltpu.roll(two, 4, 1))
        hi = jnp.where(first_half, pltpu.roll(one, 4, 1), two)
        return jnp.concatenate([lo, hi], axis=0)

    def two_heads(tr, pair):
        wide = []
        for h in (2 * pair, 2 * pair + 1):
            pieces = [jnp.zeros((h * D, Q), BF16)] if h else []
            pieces.append(tr[h * D : (h + 1) * D])
            if h < HEADS - 1:
                pieces.append(jnp.zeros((C - (h + 1) * D, Q), BF16))
            wide.append(jnp.concatenate(pieces, axis=0))
        return jnp.concatenate(wide, axis=1)

    def by_head(rows):
        return jnp.concatenate([rows * head_of[h] for h in range(HEADS)], axis=0)

    chan = lax.broadcasted_iota(jnp.int32, (1, C), 1) // D
    head_of = [(chan == h).astype(BF16) for h in range(HEADS)]

    acc_qkv[...] = jnp.zeros_like(acc_qkv)
    acc_gain[...] = jnp.zeros_like(acc_gain)
    acc_out[...] = jnp.zeros_like(acc_out)

    @pl.loop(0, NC)
    def _(t):
        c = turn(t)
        arrived(0, c, xt)

        @pl.when(t == 0)
        def _():
            halo_start(ogp, 0, OG_PIECES[0])

        chunk = rows_of(c * CP, CP)
        unit, _ = normalize(xt[chunk, :].astype(F32))
        unit_t[chunk, :] = unit
        stage[...] = (unit * gain).reshape(NF, M, C)

        @pl.loop(0, NG)
        def _(j):
            g = c * NG + j
            eight = pl.ds(pl.multiple_of(j * 8, 8), 8)
            normed = quads(stage[:, eight, :])
            n_s[g] = normed
            qkv = nn(normed, wcat).astype(BF16)
            queries, keys, values = qkv[:, :C], qkv[:, C : 2 * C], qkv[:, 2 * C :]
            q_s[g] = queries
            v_s[g] = values
            q_tr = jnp.transpose(queries)
            k_tr = jnp.transpose(keys)
            v_tr = jnp.transpose(values)
            k_t[g] = k_tr
            mixed = []
            for b in range(2):
                at = slice(b * Q, (b + 1) * Q)
                parts = []
                for pair in range(HEADS // 2):
                    s = nn(keys[at], two_heads(q_tr[:, at], pair)).reshape(Q // 8, 8, 2 * Q)
                    top = jnp.max(s, axis=0)
                    top = jnp.maximum(top, pltpu.roll(top, 4, 0))
                    e = jnp.exp2((s - top[None]) * (scale * LOG2E))
                    below = jnp.sum(e, axis=0)
                    inv = diag / (below + pltpu.roll(below, 4, 0))
                    p = (e * inv[None]).reshape(Q, 2 * Q)
                    probs[(g * 2 + b) * 2 + pair] = p
                    pb = p.astype(BF16)
                    for k in range(2):
                        h = 2 * pair + k
                        parts.append(nn(v_tr[h * D : (h + 1) * D, at], pb[:, k * Q : (k + 1) * Q]))
                mixed.append(jnp.concatenate(parts, axis=0))
            stage[:, eight, :] = from_quads(jnp.transpose(jnp.concatenate(mixed, axis=1)))

        mix_s[chunk, :] = stage[...].reshape(CP, C).astype(BF16)
        to_time(1, c, mix_s, mix_f)

        for late in (1, 2):
            if OG_PIECES[late]:
                @pl.when(t == late - 1)
                def _(late=late):
                    halo_start(ogp, 0, OG_PIECES[late])

    def middle(c):
        arrived(1, c, mix_f)
        chunk = pl.ds(c * CP, CP)
        mixed = mix_f[chunk, :]
        hidden = x_ref[chunk, :].astype(F32) + nn(mixed, wout_ref[...])
        sigma = 1.0 / (1.0 + jnp.exp(-hidden))
        act = (hidden * sigma).astype(BF16)
        ghidden = (ogp[pl.ds(W + c * CP, CP), :].astype(F32)
                   + gact[chunk, :] * sigma * (1.0 + hidden * (1.0 - sigma)))
        ghb = ghidden.astype(BF16)
        gm_s[chunk, :] = nt(ghb, wout_ref[...]).astype(BF16)
        to_time(2, c, gm_s, gm_t)
        hid[chunk, :] = hidden
        actp[pl.ds(W + c * CP, CP), :] = act
        gh[chunk, :] = ghidden
        acc_out[...] += tn(mixed, ghb)
        act_t[:, c * CP : (c + 1) * CP] = jnp.transpose(act)

    middle(1)
    halo_wait(ogp, 0)

    @pl.loop(0, 2)
    def _(k):
        grad_act_row(k * (ROWS - 1))

    middle(0)
    middle(2)

    def sum_a_send(s, size, src, dst):
        @pl.loop(1, 8)
        def _(k):
            a2, dev = a_peer(k)
            pltpu.make_async_remote_copy(
                src.at[rows_of(a2 * size, size)], dst.at[rows_of(a * size, size)],
                wsnd.at[s], wrcv.at[s], device_id=dev, device_id_type=MESH).start()

        own = rows_of(a * size, size)
        dst[own, :] = src[own, :]

    def sum_b_send(s, size, base, src, mid, dst):
        view = src.at[pl.ds(0, 7 * size)]
        pltpu.make_async_copy(view, view, wrcv.at[s - 1]).wait()
        total = src[pl.ds(0, size), :].astype(F32)
        for k in range(1, 8):
            total = total + src[pl.ds(k * size, size), :].astype(F32)
        mid[...] = total.astype(BF16)

        @pl.loop(0, size // 16)
        def _(o):
            owner = 2 * (base + o)

            @pl.when(owner != q)
            def _():
                pltpu.make_async_remote_copy(
                    mid.at[rows_of(o * 16, 16)], dst.at[rows_of(q * 16, 16)],
                    wsnd.at[s], wrcv.at[s], device_id=q_device(owner), device_id_type=MESH).start()

            @pl.when(owner == q)
            def _():
                dst[rows_of(q * 16, 16), :] = mid[rows_of(o * 16, 16), :]

    def owns(size, base):
        return jnp.logical_and(
            lax.rem(q, 2) == 0, jnp.logical_and(q >= 2 * base, q < 2 * base + size // 8))

    def sum_b_back(s, size, base, src, dst):
        @pl.when(owns(size, base))
        def _():
            view = src.at[pl.ds(0, 31 * 16)]
            pltpu.make_async_copy(view, view, wrcv.at[s - 1]).wait()
            total = jnp.sum(src[...].astype(F32).reshape(32, 16, C), axis=0) * factor
            mine = rows_of((q // 2 - base) * 16, 16)
            dst[mine, :] = total.astype(BF16)

            @pl.loop(1, 32)
            def _(k):
                pltpu.make_async_remote_copy(
                    dst.at[mine], dst.at[mine], wsnd.at[s], wrcv.at[s],
                    device_id=q_device(lax.rem(q + k, 32)), device_id_type=MESH).start()

    def sum_a_back(s, size, base, src, dst):
        nblock = size // 16

        @pl.when(owns(size, base))
        def _():
            view = src.at[pl.ds(0, (nblock - 1) * 16)]
            pltpu.make_async_copy(view, view, wrcv.at[s - 1]).wait()

        @pl.when(jnp.logical_not(owns(size, base)))
        def _():
            view = src.at[pl.ds(0, nblock * 16)]
            pltpu.make_async_copy(view, view, wrcv.at[s - 1]).wait()

        own = rows_of(a * size, size)

        @pl.loop(1, 8)
        def _(k):
            pltpu.make_async_remote_copy(
                src, dst.at[own], wsnd.at[s], wrcv.at[s], device_id=a_peer(k)[1], device_id_type=MESH).start()

        pltpu.make_async_copy(src, dst.at[own], osem.at[s // 4]).start()

    def sum_finish(s, size, base, src, mid, back, total, dst):
        own = rows_of(a * size, size)
        pltpu.make_async_copy(total, dst.at[own], osem.at[s // 4]).wait()
        view = dst.at[pl.ds(0, 7 * size)]
        pltpu.make_async_copy(view, view, wrcv.at[s + 3]).wait()
        sent = src.at[pl.ds(0, 7 * size)]
        pltpu.make_async_copy(sent, sent, wsnd.at[s]).wait()
        nblock = size // 16

        @pl.when(owns(size, base))
        def _():
            few = mid.at[pl.ds(0, (nblock - 1) * 16)]
            pltpu.make_async_copy(few, few, wsnd.at[s + 1]).wait()
            many = back.at[pl.ds(0, 31 * 16)]
            pltpu.make_async_copy(many, many, wsnd.at[s + 2]).wait()

        @pl.when(jnp.logical_not(owns(size, base)))
        def _():
            few = mid.at[pl.ds(0, nblock * 16)]
            pltpu.make_async_copy(few, few, wsnd.at[s + 1]).wait()

        pltpu.make_async_copy(view, view, wsnd.at[s + 3]).wait()

    @pl.loop(0, 2)
    def _(k):
        shift_row(k * (ROWS + 1))

    for i in range(3):
        grad = nn(act_t[...], og_sh[(2 - i) * W : (2 - i) * W + PIX, :])
        for j in range(3):
            at = (3 * i + j) * C
            e_s[at : at + C, :] = grad[:, j * C : (j + 1) * C].astype(BF16)
    e_s[9 * C : 10 * C, :] = acc_out[...].astype(BF16)

    def conv_row(row):
        total = jnp.zeros((W, 3 * C), F32)
        for i in range(3):
            wide = jnp.concatenate([wconv_ref[i, j * C : (j + 1) * C, :] for j in range(3)], axis=1)
            total = total + nn(actp[rows_of((row + i) * W, W), :], wide)
        here = rows_of(row * W, W)
        conv = before(total[:, :C]) + total[:, C : 2 * C] + after(total[:, 2 * C :])
        out_ref[here, :] = (hid[here, :] + conv).astype(BF16)

    @pl.loop(0, NC)
    def _(t):
        c = turn(t)
        arrived(2, c, gm_t)
        chunk = rows_of(c * CP, CP)
        stage[...] = gm_t[chunk, :].astype(F32).reshape(NF, M, C)

        @pl.loop(0, NG)
        def _(j):
            g = c * NG + j
            eight = pl.ds(pl.multiple_of(j * 8, 8), 8)
            gmixed = quads(stage[:, eight, :])
            gm_tr = jnp.transpose(gmixed)
            queries, values, k_tr = q_s[g], v_s[g], k_t[g]
            gqs, gks, gvs = [], [], []
            for b in range(2):
                at = slice(b * Q, (b + 1) * Q)
                parts, scores, weights = [], [], []
                for pair in range(HEADS // 2):
                    gp = nn(values[at], two_heads(gm_tr[:, at], pair)).reshape(Q // 8, 8, 2 * Q)
                    p = probs[(g * 2 + b) * 2 + pair]
                    p3 = p.reshape(Q // 8, 8, 2 * Q)
                    dot = jnp.sum(p3 * gp, axis=0)
                    dot = dot + pltpu.roll(dot, 4, 0)
                    gs = (p3 * (gp - dot[None]) * scale).reshape(Q, 2 * Q).astype(BF16)
                    for k in range(2):
                        h = 2 * pair + k
                        parts.append(nn(k_tr[h * D : (h + 1) * D, at], gs[:, k * Q : (k + 1) * Q]))
                    scores.append(gs)
                    weights.append(p.astype(BF16))
                gqs.append(jnp.concatenate(parts, axis=0))
                gks.append(nn(jnp.concatenate(scores, axis=1), by_head(queries[at])))
                gvs.append(nn(jnp.concatenate(weights, axis=1), by_head(gmixed[at])))
            gq = jnp.transpose(jnp.concatenate(gqs, axis=1))
            gk, gv = jnp.concatenate(gks, axis=0), jnp.concatenate(gvs, axis=0)
            grads = jnp.concatenate([gq.astype(BF16), gk.astype(BF16), gv.astype(BF16)], axis=1)
            stage[:, eight, :] = from_quads(nt(grads, wcat))
            acc_qkv[...] += tn(n_s[g], grads)

        gnormed = stage[...].reshape(CP, C).astype(BF16)
        gn_s[chunk, :] = gnormed
        to_time(3, c, gn_s, gn_f)
        @pl.when(t == 0)
        def _():
            sum_a_send(0, EP, e_s, e_r)

        acc_gain[...] += jnp.sum((gnormed.astype(F32) * unit_t[chunk, :]).reshape(CP // 8, 8, C), axis=0)


    for i in range(3):
        for k in range(8):
            lo = max(i * C, k * 48)
            hi = min((i + 1) * C, (k + 1) * 48)
            if lo < hi:
                at = k * LP + lo - k * 48
                l_s[at : at + hi - lo, :] = acc_qkv[lo - i * C : hi - i * C, i * C : (i + 1) * C].astype(BF16)
    total_gain = jnp.sum(acc_gain[...], axis=0, keepdims=True)
    for k in range(8):
        l_s[k * LP + 48 : (k + 1) * LP, :] = jnp.broadcast_to(total_gain, (16, C)).astype(BF16)
    sum_a_send(4, LP, l_s, l_r)
    halo_start(actp, 1, ACT_PIECES[0])

    def put_out(k, at, size):
        rows = pl.ds(at, size)
        return pltpu.make_async_copy(out_ref.at[rows], out_hbm.at[rows], osem.at[2 + k])

    @pl.loop(1, ROWS - 1)
    def _(row):
        conv_row(row)

    put_out(0, W, 2 * W).start()
    def put_gf(c):
        chunk = rows_of(c * CP, CP)
        return pltpu.make_async_copy(gf_ref.at[chunk], gf_hbm.at[chunk], osem.at[5 + c])

    def grad_frames(c):
        arrived(3, c, gn_f)
        chunk = rows_of(c * CP, CP)
        unit, inverse = normalize(x_ref[chunk, :].astype(F32))
        gscaled = gn_f[chunk, :].astype(F32) * gain
        first = jnp.mean(gscaled, axis=-1, keepdims=True)
        second = jnp.mean(gscaled * unit, axis=-1, keepdims=True)
        gf_ref[chunk, :] = (gh[chunk, :] + inverse * (gscaled - first - unit * second)).astype(BF16)
        put_gf(c).start()

    grad_frames(1)
    sum_b_send(5, LP, EB, l_r, l_b, l_br)
    sum_b_send(1, EP, 0, e_r, e_b, e_br)
    halo_start(actp, 1, ACT_PIECES[1])

    grad_frames(0)
    sum_b_back(6, LP, EB, l_br, l_g)
    sum_b_back(2, EP, 0, e_br, e_g)
    halo_start(actp, 1, ACT_PIECES[2])
    grad_frames(2)
    sum_a_back(7, LP, EB, l_g, l_f)
    sum_a_back(3, EP, 0, e_g, e_f)
    halo_wait(actp, 1)

    @pl.loop(0, 2)
    def _(k):
        conv_row(k * (ROWS - 1))

    put_out(1, 0, W).start()
    put_out(2, 3 * W, W).start()
    sum_finish(0, EP, 0, e_r, e_b, e_br, e_g, e_f)

    @pl.loop(0, NC)
    def _(c):
        left(0, c, x_ref)
        left(1, c, mix_s)
        left(2, c, gm_s)
        left(3, c, gn_s)

    for c in range(NC):
        put_gf(c).wait()
    put_out(0, W, 2 * W).wait()
    put_out(1, 0, W).wait()
    put_out(2, 3 * W, W).wait()
    sum_finish(4, LP, EB, l_r, l_b, l_br, l_g, l_f)


def finish(
    out_s, gf_s, e_h, l_h, out_h, gf_h, gain_h, qkv_h, gout_h, conv_h,
    gain, qkv, gout, conv, e_v, l_v, out_v, gf_v, sem,
):
    def put(k, src, dst):
        copy = pltpu.make_async_copy(src, dst, sem.at[k])
        copy.start()
        return copy

    early, late = put(6, e_h, e_v), put(7, l_h, l_v)
    first, second = put(8, out_s, out_v), put(9, gf_s, gf_v)
    copies = []
    early.wait()
    conv[...] = e_v[: 9 * C, :].astype(F32)
    copies.append(put(2, conv, conv_h))
    gout[...] = e_v[9 * C :, :].astype(F32)
    copies.append(put(3, gout, gout_h))
    first.wait()
    copies.append(put(0, out_v, out_h))
    second.wait()
    copies.append(put(1, gf_v, gf_h))
    late.wait()
    for k in range(8):
        qkv[k * 48 : (k + 1) * 48, :] = l_v[k * LP : k * LP + 48, :].astype(F32)
    copies.append(put(4, qkv, qkv_h))
    gain[...] = l_v[48:64, :].astype(F32)[:1]
    copies.append(put(5, gain, gain_h))
    for copy in copies:
        copy.wait()


def on_device(frames, norm_gain, qkv_weight, out_weight, conv_weight, out_grad):
    total_pixels = PIX * NF * NR
    factor = 1.0 / math.sqrt(total_pixels)
    hbm = pl.BlockSpec(memory_space=pltpu.HBM)
    sds = jax.ShapeDtypeStruct
    full = (PIX, C)
    parts = pl.pallas_call(
        lambda *refs: kernel(factor, *refs),
        out_shape=(sds(full, BF16), sds(full, BF16), sds((8 * EP, C), BF16), sds((8 * LP, C), BF16)),
        in_specs=[hbm] * 6,
        out_specs=(hbm,) * 4,
        scratch_shapes=[
            pltpu.VMEM(full, BF16),
            pltpu.VMEM((1, C), F32),
            pltpu.VMEM((3, C, C), BF16),
            pltpu.VMEM((C, C), BF16),
            pltpu.VMEM((3, 3 * C, C), BF16),
            pltpu.VMEM(full, BF16),
            pltpu.VMEM(full, F32),
            pltpu.VMEM((NF, M, C), F32),
            pltpu.VMEM((NC * NG, C, G), BF16),
            pltpu.VMEM((NC * NG, G, C), BF16),
            pltpu.VMEM((NC * NG, G, C), BF16),
            pltpu.VMEM((NC * NG, G, C), BF16),
            pltpu.VMEM((NC * NG * HEADS, Q, 2 * Q), F32),
            pltpu.VMEM(full, BF16),
            pltpu.VMEM(full, BF16),
            pltpu.VMEM(full, BF16),
            pltpu.VMEM(full, BF16),
            pltpu.VMEM(full, BF16),
            pltpu.VMEM(full, BF16),
            pltpu.VMEM(full, BF16),
            pltpu.VMEM(full, BF16),
            pltpu.VMEM((PIX + 2 * W, C), BF16),
            pltpu.VMEM((PIX + 2 * W, C), BF16),
            pltpu.VMEM(full, F32),
            pltpu.VMEM(full, F32),
            pltpu.VMEM(full, F32),
            pltpu.VMEM((C, PIX), BF16),
            pltpu.VMEM((PIX + 2 * W, 3 * C), BF16),
            pltpu.VMEM((C, 3 * C), F32),
            pltpu.VMEM((8, C), F32),
            pltpu.VMEM((C, C), F32),
            pltpu.VMEM((8 * EP, C), BF16),
            pltpu.VMEM((8 * EP, C), BF16),
            pltpu.VMEM((EP, C), BF16),
            pltpu.VMEM((32 * 16, C), BF16),
            pltpu.VMEM((EP, C), BF16),
            pltpu.VMEM((8 * LP, C), BF16),
            pltpu.VMEM((8 * LP, C), BF16),
            pltpu.VMEM((LP, C), BF16),
            pltpu.VMEM((32 * 16, C), BF16),
            pltpu.VMEM((LP, C), BF16),
            pltpu.SemaphoreType.DMA((6,)),
            pltpu.SemaphoreType.DMA((8,)),
            pltpu.SemaphoreType.DMA((4, NC)),
            pltpu.SemaphoreType.DMA((4, NC)),
            pltpu.SemaphoreType.DMA((2, 2, 3)),
            pltpu.SemaphoreType.DMA((2, 2, 3)),
            pltpu.SemaphoreType.DMA((8,)),
            pltpu.SemaphoreType.DMA((8,)),
        ],
        compiler_params=pltpu.CompilerParams(
            collective_id=0, has_side_effects=True, vmem_limit_bytes=60 << 20
        ),
        name="block",
    )(
        frames.reshape(full),
        norm_gain.reshape(1, C),
        qkv_weight,
        out_weight,
        conv_weight.reshape(3, 3 * C, C),
        out_grad.reshape(full),
    )
    sizes = (sds(full, BF16), sds(full, BF16), sds((1, C), F32),
             sds((3 * C, C), F32), sds((C, C), F32), sds((9 * C, C), F32))
    outs = pl.pallas_call(
        finish,
        out_shape=sizes,
        in_specs=[hbm] * 4,
        out_specs=(hbm,) * 6,
        scratch_shapes=[pltpu.VMEM(s.shape, F32) for s in sizes[2:]] + [
            pltpu.VMEM((8 * EP, C), BF16), pltpu.VMEM((8 * LP, C), BF16),
            pltpu.VMEM(full, BF16), pltpu.VMEM(full, BF16), pltpu.SemaphoreType.DMA((10,))],
        compiler_params=pltpu.CompilerParams(vmem_limit_bytes=60 << 20),
        name="finish",
    )(*parts)
    output, grad_frames, grad_gain, grad_qkv, grad_out, grad_conv = outs
    return (
        output.reshape(frames.shape),
        grad_frames.reshape(frames.shape),
        grad_gain.reshape(C),
        grad_qkv.reshape(3, C, C),
        grad_out,
        grad_conv.reshape(3, 3, C, C),
    )


def solution(mesh):
    return jax.shard_map(
        on_device,
        mesh=mesh,
        in_specs=(P("frame", "row", None, None), P(), P(), P(), P(), P("frame", "row", None, None)),
        out_specs=(
            P("frame", "row", None, None),
            P("frame", "row", None, None),
            P(),
            P(),
            P(),
            P(),
        ),
        check_vma=False,
    )
```

```python
import math

import jax
import jax.numpy as jnp
from jax import lax
from jax.experimental import pallas as pl
from jax.experimental.pallas import tpu as pltpu
from jax.sharding import PartitionSpec as P

HEADS = 4
EPSILON = 1e-05
MESH = pl.DeviceIdType.MESH
F32 = jnp.float32
BF16 = jnp.bfloat16

NF = 32
NR = 8
C = 128
D = C // HEADS
ROWS = 4
W = 384
PIX = ROWS * W
NC = 3
CP = PIX // NC
M = CP // NF
NG = M // 8
G = 8 * NF
Q = G // 2
LOG2E = math.log2(math.e)

EP = 160
LP = 64
EB = EP // 16
ACT_PIECES = ((0, 1), (2,), ())
OG_PIECES = ((), (0, 1), (2,))


def nn(a, b):
    return jnp.dot(a, b, preferred_element_type=F32)


def nt(a, b):
    return lax.dot_general(a, b, (((1,), (1,)), ((), ())), preferred_element_type=F32)


def tn(a, b):
    return lax.dot_general(a, b, (((0,), (0,)), ((), ())), preferred_element_type=F32)


def rows_of(start, size):
    return pl.ds(pl.multiple_of(start, size), size)


def normalize(values):
    center = jnp.mean(values, axis=-1, keepdims=True)
    spread = jnp.mean(jnp.square(values - center), axis=-1, keepdims=True)
    inverse = lax.rsqrt(spread + EPSILON)
    return (values - center) * inverse, inverse


def kernel(
    factor,
    x_hbm, gain_hbm, wqkv_hbm, wout_hbm, wconv_hbm, og_hbm,
    out_hbm, gf_hbm, e_f, l_f,
    x_ref, gain_ref, wqkv_ref, wout_ref, wconv_ref,
    xt, unit_t, stage, k_t, v_s, q_s, n_s, probs,
    mix_s, mix_f, gm_s, gm_t, gn_s, gn_f, out_ref, gf_ref,
    ogp, actp, gact, hid, gh, act_t, og_sh,
    acc_qkv, acc_gain, acc_out,
    e_s, e_r, e_b, e_br, e_g,
    l_s, l_r, l_b, l_br, l_g,
    isem, osem, snd, rcv, hsnd, hrcv, wsnd, wrcv,
):
    f = lax.axis_index("frame")
    r = lax.axis_index("row")
    core = lax.rem(f, 2)
    fx = f // 2
    y = r // 2
    zh = lax.rem(r, 2)
    a = y * 2 + core
    q = zh * 16 + fx

    def frame_peer(k):
        return lax.rem(f + k, NF)

    def a_peer(k):
        a2 = lax.rem(a + k, 8)
        return a2, (fx * 2 + lax.rem(a2, 2), (a2 // 2) * 2 + zh)

    def q_device(q2):
        return (lax.rem(q2, 16) * 2 + core, y * 2 + q2 // 16)

    barrier = pltpu.get_barrier_semaphore()

    fetches = [
        pltpu.make_async_copy(src, dst, isem.at[k])
        for k, (src, dst) in enumerate([
            (x_hbm, x_ref), (gain_hbm, gain_ref), (wqkv_hbm, wqkv_ref), (wout_hbm, wout_ref),
            (wconv_hbm, wconv_ref), (og_hbm, ogp.at[pl.ds(W, PIX)]),
        ])
    ]
    for fetch in fetches:
        fetch.start()

    @pl.loop(1, NF, unroll=True)
    def _(k):
        pl.semaphore_signal(barrier, inc=1, device_id=(frame_peer(k), r), device_id_type=MESH)

    @pl.loop(0, 16, unroll=True)
    def _(k):
        pl.semaphore_signal(barrier, inc=1, device_id=(k * 2 + core, y * 2 + 1 - zh), device_id_type=MESH)

    @pl.loop(2, 8, unroll=True)
    def _(k):
        a2 = lax.rem(y * 2 + k, 8)
        pl.semaphore_signal(
            barrier, inc=1, device_id=(fx * 2 + lax.rem(a2, 2), (a2 // 2) * 2 + zh), device_id_type=MESH)

    @pl.when(r > 0)
    def _():
        pl.semaphore_signal(barrier, inc=1, device_id=(f, r - 1), device_id_type=MESH)

    @pl.when(r < NR - 1)
    def _():
        pl.semaphore_signal(barrier, inc=1, device_id=(f, r + 1), device_id_type=MESH)

    col = lax.broadcasted_iota(jnp.int32, (W, C), 0)
    first_col = col == 0
    last_col = col == W - 1

    def after(z):
        return jnp.where(last_col, 0.0, pltpu.roll(z, W - 1, 0))

    def before(z):
        return jnp.where(first_col, 0.0, pltpu.roll(z, 1, 0))

    def shift_row(row):
        here = rows_of(row * W, W)
        own = ogp[here, :]
        wide = own.astype(F32)
        og_sh[here, :] = jnp.concatenate([after(wide).astype(BF16), own, before(wide).astype(BF16)], axis=1)

    def grad_act_row(row):
        total = jnp.zeros((W, 3 * C), F32)
        for i in range(3):
            total = total + nt(ogp[rows_of((row + 2 - i) * W, W), :], wconv_ref[i])
        gact[rows_of(row * W, W), :] = (
            after(total[:, :C]) + total[:, C : 2 * C] + before(total[:, 2 * C :]))

    for fetch in fetches:
        fetch.wait()

    @pl.loop(1, ROWS - 1)
    def _(row):
        grad_act_row(row)

    @pl.loop(1, ROWS + 1)
    def _(row):
        shift_row(row)

    pl.semaphore_wait(barrier, 31 + 16 + 6 + jnp.where(r > 0, 1, 0) + jnp.where(r < NR - 1, 1, 0))

    def to_time(phase, c, src, dst):
        @pl.loop(1, NF, unroll=True)
        def _(k):
            d = frame_peer(k)
            pltpu.make_async_remote_copy(
                src.at[rows_of(c * CP + d * M, M)], dst.at[rows_of(c * CP + f * M, M)],
                snd.at[phase, c], rcv.at[phase, c], device_id=(d, r), device_id_type=MESH,
            ).start()

        own = rows_of(c * CP + f * M, M)
        dst[own, :] = src[own, :]

    def arrived(phase, c, dst):
        view = dst.at[pl.ds(pl.multiple_of(c * CP, M), (NF - 1) * M)]
        pltpu.make_async_copy(view, view, rcv.at[phase, c]).wait()

    def left(phase, c, src):
        view = src.at[pl.ds(pl.multiple_of(c * CP, M), (NF - 1) * M)]
        pltpu.make_async_copy(view, view, snd.at[phase, c]).wait()

    def turn(t):
        return lax.rem(NC + 1 - t, NC)

    @pl.loop(0, NC)
    def _(t):
        to_time(0, turn(t), x_ref, xt)

    def halo_up(buf, s, piece):
        return pltpu.make_async_remote_copy(
            buf.at[pl.ds(W + piece * C, C)], buf.at[pl.ds(5 * W + piece * C, C)],
            hsnd.at[s, 0, piece], hrcv.at[s, 0, piece], device_id=(f, r - 1), device_id_type=MESH)

    def halo_down(buf, s, piece):
        return pltpu.make_async_remote_copy(
            buf.at[pl.ds(4 * W + piece * C, C)], buf.at[pl.ds(piece * C, C)],
            hsnd.at[s, 1, piece], hrcv.at[s, 1, piece], device_id=(f, r + 1), device_id_type=MESH)

    def halo_start(buf, s, pieces):
        @pl.when(r > 0)
        def _():
            for piece in pieces:
                halo_up(buf, s, piece).start()

        @pl.when(r < NR - 1)
        def _():
            for piece in pieces:
                halo_down(buf, s, piece).start()

    edge = jnp.zeros((W, C), BF16)

    @pl.when(r == 0)
    def _():
        ogp[pl.ds(0, W), :] = edge
        actp[pl.ds(0, W), :] = edge

    @pl.when(r == NR - 1)
    def _():
        ogp[pl.ds(5 * W, W), :] = edge
        actp[pl.ds(5 * W, W), :] = edge

    def halo_wait(buf, s):
        @pl.when(r > 0)
        def _():
            for piece in range(3):
                halo_up(buf, s, piece).wait_send()
                halo_down(buf, s, piece).wait_recv()

        @pl.when(r < NR - 1)
        def _():
            for piece in range(3):
                halo_down(buf, s, piece).wait_send()
                halo_up(buf, s, piece).wait_recv()

    gain = gain_ref[...]
    wcat = jnp.concatenate([wqkv_ref[0], wqkv_ref[1], wqkv_ref[2]], axis=1)
    scale = D ** (-0.5)
    sub = lax.broadcasted_iota(jnp.int32, (8, 2 * Q), 0)
    lane = lax.broadcasted_iota(jnp.int32, (8, 2 * Q), 1)
    diag = (lax.rem(sub, 4) == lax.rem(lane, 4)).astype(F32)
    first_half = lax.broadcasted_iota(jnp.int32, (NF // 2, 8, C), 1) < 4

    def quads(rows):
        lo, hi = rows[: NF // 2], rows[NF // 2 :]
        one = jnp.where(first_half, lo, pltpu.roll(hi, 4, 1)).reshape(Q, C)
        two = jnp.where(first_half, pltpu.roll(lo, 4, 1), hi).reshape(Q, C)
        return jnp.concatenate([one, two], axis=0).astype(BF16)

    def from_quads(rows):
        one = rows[:Q].reshape(NF // 2, 8, C)
        two = rows[Q:].reshape(NF // 2, 8, C)
        lo = jnp.where(first_half, one, pltpu.roll(two, 4, 1))
        hi = jnp.where(first_half, pltpu.roll(one, 4, 1), two)
        return jnp.concatenate([lo, hi], axis=0)

    def two_heads(tr, pair):
        wide = []
        for h in (2 * pair, 2 * pair + 1):
            pieces = [jnp.zeros((h * D, Q), BF16)] if h else []
            pieces.append(tr[h * D : (h + 1) * D])
            if h < HEADS - 1:
                pieces.append(jnp.zeros((C - (h + 1) * D, Q), BF16))
            wide.append(jnp.concatenate(pieces, axis=0))
        return jnp.concatenate(wide, axis=1)

    def by_head(rows):
        return jnp.concatenate([rows * head_of[h] for h in range(HEADS)], axis=0)

    chan = lax.broadcasted_iota(jnp.int32, (1, C), 1) // D
    head_of = [(chan == h).astype(BF16) for h in range(HEADS)]

    acc_qkv[...] = jnp.zeros_like(acc_qkv)
    acc_gain[...] = jnp.zeros_like(acc_gain)
    acc_out[...] = jnp.zeros_like(acc_out)

    @pl.loop(0, NC)
    def _(t):
        c = turn(t)
        arrived(0, c, xt)

        @pl.when(t == 0)
        def _():
            halo_start(ogp, 0, OG_PIECES[0])

        chunk = rows_of(c * CP, CP)
        unit, _ = normalize(xt[chunk, :].astype(F32))
        unit_t[chunk, :] = unit
        stage[...] = (unit * gain).reshape(NF, M, C)

        @pl.loop(0, NG)
        def _(j):
            g = c * NG + j
            eight = pl.ds(pl.multiple_of(j * 8, 8), 8)
            normed = quads(stage[:, eight, :])
            n_s[g] = normed
            qkv = nn(normed, wcat).astype(BF16)
            queries, keys, values = qkv[:, :C], qkv[:, C : 2 * C], qkv[:, 2 * C :]
            q_s[g] = queries
            v_s[g] = values
            q_tr = jnp.transpose(queries)
            k_tr = jnp.transpose(keys)
            v_tr = jnp.transpose(values)
            k_t[g] = k_tr
            mixed = []
            for b in range(2):
                at = slice(b * Q, (b + 1) * Q)
                parts = []
                for pair in range(HEADS // 2):
                    s = nn(keys[at], two_heads(q_tr[:, at], pair)).reshape(Q // 8, 8, 2 * Q)
                    top = jnp.max(s, axis=0)
                    top = jnp.maximum(top, pltpu.roll(top, 4, 0))
                    e = jnp.exp2((s - top[None]) * (scale * LOG2E))
                    below = jnp.sum(e, axis=0)
                    inv = diag / (below + pltpu.roll(below, 4, 0))
                    p = (e * inv[None]).reshape(Q, 2 * Q)
                    probs[(g * 2 + b) * 2 + pair] = p
                    pb = p.astype(BF16)
                    for k in range(2):
                        h = 2 * pair + k
                        parts.append(nn(v_tr[h * D : (h + 1) * D, at], pb[:, k * Q : (k + 1) * Q]))
                mixed.append(jnp.concatenate(parts, axis=0))
            stage[:, eight, :] = from_quads(jnp.transpose(jnp.concatenate(mixed, axis=1)))

        mix_s[chunk, :] = stage[...].reshape(CP, C).astype(BF16)
        to_time(1, c, mix_s, mix_f)

        for late in (1, 2):
            if OG_PIECES[late]:
                @pl.when(t == late - 1)
                def _(late=late):
                    halo_start(ogp, 0, OG_PIECES[late])

    def middle(c):
        arrived(1, c, mix_f)
        chunk = pl.ds(c * CP, CP)
        mixed = mix_f[chunk, :]
        hidden = x_ref[chunk, :].astype(F32) + nn(mixed, wout_ref[...])
        sigma = 1.0 / (1.0 + jnp.exp(-hidden))
        act = (hidden * sigma).astype(BF16)
        ghidden = (ogp[pl.ds(W + c * CP, CP), :].astype(F32)
                   + gact[chunk, :] * sigma * (1.0 + hidden * (1.0 - sigma)))
        ghb = ghidden.astype(BF16)
        gm_s[chunk, :] = nt(ghb, wout_ref[...]).astype(BF16)
        to_time(2, c, gm_s, gm_t)
        hid[chunk, :] = hidden
        actp[pl.ds(W + c * CP, CP), :] = act
        gh[chunk, :] = ghidden
        acc_out[...] += tn(mixed, ghb)
        act_t[:, c * CP : (c + 1) * CP] = jnp.transpose(act)

    middle(1)
    halo_wait(ogp, 0)

    @pl.loop(0, 2)
    def _(k):
        grad_act_row(k * (ROWS - 1))

    middle(0)
    middle(2)

    def sum_a_send(s, size, src, dst):
        @pl.loop(1, 8)
        def _(k):
            a2, dev = a_peer(k)
            pltpu.make_async_remote_copy(
                src.at[rows_of(a2 * size, size)], dst.at[rows_of(a * size, size)],
                wsnd.at[s], wrcv.at[s], device_id=dev, device_id_type=MESH).start()

        own = rows_of(a * size, size)
        dst[own, :] = src[own, :]

    def sum_b_send(s, size, base, src, mid, dst):
        view = src.at[pl.ds(0, 7 * size)]
        pltpu.make_async_copy(view, view, wrcv.at[s - 1]).wait()
        total = src[pl.ds(0, size), :].astype(F32)
        for k in range(1, 8):
            total = total + src[pl.ds(k * size, size), :].astype(F32)
        mid[...] = total.astype(BF16)

        @pl.loop(0, size // 16)
        def _(o):
            owner = 2 * (base + o)

            @pl.when(owner != q)
            def _():
                pltpu.make_async_remote_copy(
                    mid.at[rows_of(o * 16, 16)], dst.at[rows_of(q * 16, 16)],
                    wsnd.at[s], wrcv.at[s], device_id=q_device(owner), device_id_type=MESH).start()

            @pl.when(owner == q)
            def _():
                dst[rows_of(q * 16, 16), :] = mid[rows_of(o * 16, 16), :]

    def owns(size, base):
        return jnp.logical_and(
            lax.rem(q, 2) == 0, jnp.logical_and(q >= 2 * base, q < 2 * base + size // 8))

    def sum_b_back(s, size, base, src, dst):
        @pl.when(owns(size, base))
        def _():
            view = src.at[pl.ds(0, 31 * 16)]
            pltpu.make_async_copy(view, view, wrcv.at[s - 1]).wait()
            total = jnp.sum(src[...].astype(F32).reshape(32, 16, C), axis=0) * factor
            mine = rows_of((q // 2 - base) * 16, 16)
            dst[mine, :] = total.astype(BF16)

            @pl.loop(1, 32)
            def _(k):
                pltpu.make_async_remote_copy(
                    dst.at[mine], dst.at[mine], wsnd.at[s], wrcv.at[s],
                    device_id=q_device(lax.rem(q + k, 32)), device_id_type=MESH).start()

    def sum_a_back(s, size, base, src, dst):
        nblock = size // 16

        @pl.when(owns(size, base))
        def _():
            view = src.at[pl.ds(0, (nblock - 1) * 16)]
            pltpu.make_async_copy(view, view, wrcv.at[s - 1]).wait()

        @pl.when(jnp.logical_not(owns(size, base)))
        def _():
            view = src.at[pl.ds(0, nblock * 16)]
            pltpu.make_async_copy(view, view, wrcv.at[s - 1]).wait()

        own = rows_of(a * size, size)

        @pl.loop(1, 8)
        def _(k):
            pltpu.make_async_remote_copy(
                src, dst.at[own], wsnd.at[s], wrcv.at[s], device_id=a_peer(k)[1], device_id_type=MESH).start()

        pltpu.make_async_copy(src, dst.at[own], osem.at[s // 4]).start()

    def sum_finish(s, size, base, src, mid, back, total, dst):
        own = rows_of(a * size, size)
        pltpu.make_async_copy(total, dst.at[own], osem.at[s // 4]).wait()
        view = dst.at[pl.ds(0, 7 * size)]
        pltpu.make_async_copy(view, view, wrcv.at[s + 3]).wait()
        sent = src.at[pl.ds(0, 7 * size)]
        pltpu.make_async_copy(sent, sent, wsnd.at[s]).wait()
        nblock = size // 16

        @pl.when(owns(size, base))
        def _():
            few = mid.at[pl.ds(0, (nblock - 1) * 16)]
            pltpu.make_async_copy(few, few, wsnd.at[s + 1]).wait()
            many = back.at[pl.ds(0, 31 * 16)]
            pltpu.make_async_copy(many, many, wsnd.at[s + 2]).wait()

        @pl.when(jnp.logical_not(owns(size, base)))
        def _():
            few = mid.at[pl.ds(0, nblock * 16)]
            pltpu.make_async_copy(few, few, wsnd.at[s + 1]).wait()

        pltpu.make_async_copy(view, view, wsnd.at[s + 3]).wait()

    @pl.loop(0, 2)
    def _(k):
        shift_row(k * (ROWS + 1))

    for i in range(3):
        grad = nn(act_t[...], og_sh[(2 - i) * W : (2 - i) * W + PIX, :])
        for j in range(3):
            at = (3 * i + j) * C
            e_s[at : at + C, :] = grad[:, j * C : (j + 1) * C].astype(BF16)
    e_s[9 * C : 10 * C, :] = acc_out[...].astype(BF16)

    def conv_row(row):
        total = jnp.zeros((W, 3 * C), F32)
        for i in range(3):
            wide = jnp.concatenate([wconv_ref[i, j * C : (j + 1) * C, :] for j in range(3)], axis=1)
            total = total + nn(actp[rows_of((row + i) * W, W), :], wide)
        here = rows_of(row * W, W)
        conv = before(total[:, :C]) + total[:, C : 2 * C] + after(total[:, 2 * C :])
        out_ref[here, :] = (hid[here, :] + conv).astype(BF16)

    @pl.loop(0, NC)
    def _(t):
        c = turn(t)
        arrived(2, c, gm_t)
        chunk = rows_of(c * CP, CP)
        stage[...] = gm_t[chunk, :].astype(F32).reshape(NF, M, C)

        @pl.loop(0, NG)
        def _(j):
            g = c * NG + j
            eight = pl.ds(pl.multiple_of(j * 8, 8), 8)
            gmixed = quads(stage[:, eight, :])
            gm_tr = jnp.transpose(gmixed)
            queries, values, k_tr = q_s[g], v_s[g], k_t[g]
            gqs, gks, gvs = [], [], []
            for b in range(2):
                at = slice(b * Q, (b + 1) * Q)
                parts, scores, weights = [], [], []
                for pair in range(HEADS // 2):
                    gp = nn(values[at], two_heads(gm_tr[:, at], pair)).reshape(Q // 8, 8, 2 * Q)
                    p = probs[(g * 2 + b) * 2 + pair]
                    p3 = p.reshape(Q // 8, 8, 2 * Q)
                    dot = jnp.sum(p3 * gp, axis=0)
                    dot = dot + pltpu.roll(dot, 4, 0)
                    gs = (p3 * (gp - dot[None]) * scale).reshape(Q, 2 * Q).astype(BF16)
                    for k in range(2):
                        h = 2 * pair + k
                        parts.append(nn(k_tr[h * D : (h + 1) * D, at], gs[:, k * Q : (k + 1) * Q]))
                    scores.append(gs)
                    weights.append(p.astype(BF16))
                gqs.append(jnp.concatenate(parts, axis=0))
                gks.append(nn(jnp.concatenate(scores, axis=1), by_head(queries[at])))
                gvs.append(nn(jnp.concatenate(weights, axis=1), by_head(gmixed[at])))
            gq = jnp.transpose(jnp.concatenate(gqs, axis=1))
            gk, gv = jnp.concatenate(gks, axis=0), jnp.concatenate(gvs, axis=0)
            grads = jnp.concatenate([gq.astype(BF16), gk.astype(BF16), gv.astype(BF16)], axis=1)
            stage[:, eight, :] = from_quads(nt(grads, wcat))
            acc_qkv[...] += tn(n_s[g], grads)

        gnormed = stage[...].reshape(CP, C).astype(BF16)
        gn_s[chunk, :] = gnormed
        to_time(3, c, gn_s, gn_f)
        @pl.when(t == 0)
        def _():
            sum_a_send(0, EP, e_s, e_r)

        acc_gain[...] += jnp.sum((gnormed.astype(F32) * unit_t[chunk, :]).reshape(CP // 8, 8, C), axis=0)


    for i in range(3):
        for k in range(8):
            lo = max(i * C, k * 48)
            hi = min((i + 1) * C, (k + 1) * 48)
            if lo < hi:
                at = k * LP + lo - k * 48
                l_s[at : at + hi - lo, :] = acc_qkv[lo - i * C : hi - i * C, i * C : (i + 1) * C].astype(BF16)
    total_gain = jnp.sum(acc_gain[...], axis=0, keepdims=True)
    for k in range(8):
        l_s[k * LP + 48 : (k + 1) * LP, :] = jnp.broadcast_to(total_gain, (16, C)).astype(BF16)
    sum_a_send(4, LP, l_s, l_r)
    halo_start(actp, 1, ACT_PIECES[0])

    def put_out(k, at, size):
        rows = pl.ds(at, size)
        return pltpu.make_async_copy(out_ref.at[rows], out_hbm.at[rows], osem.at[2 + k])

    @pl.loop(1, ROWS - 1)
    def _(row):
        conv_row(row)

    put_out(0, W, 2 * W).start()
    def put_gf(c):
        chunk = rows_of(c * CP, CP)
        return pltpu.make_async_copy(gf_ref.at[chunk], gf_hbm.at[chunk], osem.at[5 + c])

    def grad_frames(c):
        arrived(3, c, gn_f)
        chunk = rows_of(c * CP, CP)
        unit, inverse = normalize(x_ref[chunk, :].astype(F32))
        gscaled = gn_f[chunk, :].astype(F32) * gain
        first = jnp.mean(gscaled, axis=-1, keepdims=True)
        second = jnp.mean(gscaled * unit, axis=-1, keepdims=True)
        gf_ref[chunk, :] = (gh[chunk, :] + inverse * (gscaled - first - unit * second)).astype(BF16)
        put_gf(c).start()

    grad_frames(1)
    sum_b_send(5, LP, EB, l_r, l_b, l_br)
    sum_b_send(1, EP, 0, e_r, e_b, e_br)
    halo_start(actp, 1, ACT_PIECES[1])

    grad_frames(0)
    sum_b_back(6, LP, EB, l_br, l_g)
    sum_b_back(2, EP, 0, e_br, e_g)
    halo_start(actp, 1, ACT_PIECES[2])
    grad_frames(2)
    sum_a_back(7, LP, EB, l_g, l_f)
    sum_a_back(3, EP, 0, e_g, e_f)
    halo_wait(actp, 1)

    @pl.loop(0, 2)
    def _(k):
        conv_row(k * (ROWS - 1))

    put_out(1, 0, W).start()
    put_out(2, 3 * W, W).start()
    sum_finish(0, EP, 0, e_r, e_b, e_br, e_g, e_f)

    @pl.loop(0, NC)
    def _(c):
        left(0, c, x_ref)
        left(1, c, mix_s)
        left(2, c, gm_s)
        left(3, c, gn_s)

    for c in range(NC):
        put_gf(c).wait()
    put_out(0, W, 2 * W).wait()
    put_out(1, 0, W).wait()
    put_out(2, 3 * W, W).wait()
    sum_finish(4, LP, EB, l_r, l_b, l_br, l_g, l_f)


def finish(
    out_s, gf_s, e_h, l_h, out_h, gf_h, gain_h, qkv_h, gout_h, conv_h,
    gain, qkv, gout, conv, e_v, l_v, out_v, gf_v, sem,
):
    def put(k, src, dst):
        copy = pltpu.make_async_copy(src, dst, sem.at[k])
        copy.start()
        return copy

    early, late = put(6, e_h, e_v), put(7, l_h, l_v)
    first, second = put(8, out_s, out_v), put(9, gf_s, gf_v)
    copies = []
    early.wait()
    conv[...] = e_v[: 9 * C, :].astype(F32)
    copies.append(put(2, conv, conv_h))
    gout[...] = e_v[9 * C :, :].astype(F32)
    copies.append(put(3, gout, gout_h))
    first.wait()
    copies.append(put(0, out_v, out_h))
    second.wait()
    copies.append(put(1, gf_v, gf_h))
    late.wait()
    for k in range(8):
        qkv[k * 48 : (k + 1) * 48, :] = l_v[k * LP : k * LP + 48, :].astype(F32)
    copies.append(put(4, qkv, qkv_h))
    gain[...] = l_v[48:64, :].astype(F32)[:1]
    copies.append(put(5, gain, gain_h))
    for copy in copies:
        copy.wait()


def on_device(frames, norm_gain, qkv_weight, out_weight, conv_weight, out_grad):
    total_pixels = PIX * NF * NR
    factor = 1.0 / math.sqrt(total_pixels)
    hbm = pl.BlockSpec(memory_space=pltpu.HBM)
    sds = jax.ShapeDtypeStruct
    full = (PIX, C)
    parts = pl.pallas_call(
        lambda *refs: kernel(factor, *refs),
        out_shape=(sds(full, BF16), sds(full, BF16), sds((8 * EP, C), BF16), sds((8 * LP, C), BF16)),
        in_specs=[hbm] * 6,
        out_specs=(hbm,) * 4,
        scratch_shapes=[
            pltpu.VMEM(full, BF16),
            pltpu.VMEM((1, C), F32),
            pltpu.VMEM((3, C, C), BF16),
            pltpu.VMEM((C, C), BF16),
            pltpu.VMEM((3, 3 * C, C), BF16),
            pltpu.VMEM(full, BF16),
            pltpu.VMEM(full, F32),
            pltpu.VMEM((NF, M, C), F32),
            pltpu.VMEM((NC * NG, C, G), BF16),
            pltpu.VMEM((NC * NG, G, C), BF16),
            pltpu.VMEM((NC * NG, G, C), BF16),
            pltpu.VMEM((NC * NG, G, C), BF16),
            pltpu.VMEM((NC * NG * HEADS, Q, 2 * Q), F32),
            pltpu.VMEM(full, BF16),
            pltpu.VMEM(full, BF16),
            pltpu.VMEM(full, BF16),
            pltpu.VMEM(full, BF16),
            pltpu.VMEM(full, BF16),
            pltpu.VMEM(full, BF16),
            pltpu.VMEM(full, BF16),
            pltpu.VMEM(full, BF16),
            pltpu.VMEM((PIX + 2 * W, C), BF16),
            pltpu.VMEM((PIX + 2 * W, C), BF16),
            pltpu.VMEM(full, F32),
            pltpu.VMEM(full, F32),
            pltpu.VMEM(full, F32),
            pltpu.VMEM((C, PIX), BF16),
            pltpu.VMEM((PIX + 2 * W, 3 * C), BF16),
            pltpu.VMEM((C, 3 * C), F32),
            pltpu.VMEM((8, C), F32),
            pltpu.VMEM((C, C), F32),
            pltpu.VMEM((8 * EP, C), BF16),
            pltpu.VMEM((8 * EP, C), BF16),
            pltpu.VMEM((EP, C), BF16),
            pltpu.VMEM((32 * 16, C), BF16),
            pltpu.VMEM((EP, C), BF16),
            pltpu.VMEM((8 * LP, C), BF16),
            pltpu.VMEM((8 * LP, C), BF16),
            pltpu.VMEM((LP, C), BF16),
            pltpu.VMEM((32 * 16, C), BF16),
            pltpu.VMEM((LP, C), BF16),
            pltpu.SemaphoreType.DMA((6,)),
            pltpu.SemaphoreType.DMA((8,)),
            pltpu.SemaphoreType.DMA((4, NC)),
            pltpu.SemaphoreType.DMA((4, NC)),
            pltpu.SemaphoreType.DMA((2, 2, 3)),
            pltpu.SemaphoreType.DMA((2, 2, 3)),
            pltpu.SemaphoreType.DMA((8,)),
            pltpu.SemaphoreType.DMA((8,)),
        ],
        compiler_params=pltpu.CompilerParams(
            collective_id=0, has_side_effects=True, vmem_limit_bytes=60 << 20
        ),
        name="block",
    )(
        frames.reshape(full),
        norm_gain.reshape(1, C),
        qkv_weight,
        out_weight,
        conv_weight.reshape(3, 3 * C, C),
        out_grad.reshape(full),
    )
    sizes = (sds(full, BF16), sds(full, BF16), sds((1, C), F32),
             sds((3 * C, C), F32), sds((C, C), F32), sds((9 * C, C), F32))
    outs = pl.pallas_call(
        finish,
        out_shape=sizes,
        in_specs=[hbm] * 4,
        out_specs=(hbm,) * 6,
        scratch_shapes=[pltpu.VMEM(s.shape, F32) for s in sizes[2:]] + [
            pltpu.VMEM((8 * EP, C), BF16), pltpu.VMEM((8 * LP, C), BF16),
            pltpu.VMEM(full, BF16), pltpu.VMEM(full, BF16), pltpu.SemaphoreType.DMA((10,))],
        compiler_params=pltpu.CompilerParams(vmem_limit_bytes=60 << 20),
        name="finish",
    )(*parts)
    output, grad_frames, grad_gain, grad_qkv, grad_out, grad_conv = outs
    return (
        output.reshape(frames.shape),
        grad_frames.reshape(frames.shape),
        grad_gain.reshape(C),
        grad_qkv.reshape(3, C, C),
        grad_out,
        grad_conv.reshape(3, 3, C, C),
    )


def solution(mesh):
    return jax.shard_map(
        on_device,
        mesh=mesh,
        in_specs=(P("frame", "row", None, None), P(), P(), P(), P(), P("frame", "row", None, None)),
        out_specs=(
            P("frame", "row", None, None),
            P("frame", "row", None, None),
            P(),
            P(),
            P(),
            P(),
        ),
        check_vma=False,
    )
```

```python
import math

import jax
import jax.numpy as jnp
from jax import lax
from jax.experimental import pallas as pl
from jax.experimental.pallas import tpu as pltpu
from jax.sharding import PartitionSpec as P

HEADS = 4
EPSILON = 1e-05
MESH = pl.DeviceIdType.MESH
F32 = jnp.float32
BF16 = jnp.bfloat16

NF = 32
NR = 8
C = 128
D = C // HEADS
ROWS = 4
W = 384
PIX = ROWS * W
NC = 3
CP = PIX // NC
M = CP // NF
NG = M // 8
G = 8 * NF
Q = G // 2
LOG2E = math.log2(math.e)

EP = 160
LP = 64
EB = EP // 16
ACT_PIECES = ((0,), (1, 2), ())
OG_PIECES = ((), (0, 1, 2), ())


def nn(a, b):
    return jnp.dot(a, b, preferred_element_type=F32)


def nt(a, b):
    return lax.dot_general(a, b, (((1,), (1,)), ((), ())), preferred_element_type=F32)


def tn(a, b):
    return lax.dot_general(a, b, (((0,), (0,)), ((), ())), preferred_element_type=F32)


def rows_of(start, size):
    return pl.ds(pl.multiple_of(start, size), size)


def normalize(values):
    center = jnp.mean(values, axis=-1, keepdims=True)
    spread = jnp.mean(jnp.square(values - center), axis=-1, keepdims=True)
    inverse = lax.rsqrt(spread + EPSILON)
    return (values - center) * inverse, inverse


def kernel(
    factor,
    x_hbm, gain_hbm, wqkv_hbm, wout_hbm, wconv_hbm, og_hbm,
    out_hbm, gf_hbm, e_f, l_f,
    x_ref, gain_ref, wqkv_ref, wout_ref, wconv_ref,
    xt, unit_t, stage, k_t, v_s, q_s, n_s, probs,
    mix_s, mix_f, gm_s, gm_t, gn_s, gn_f, out_ref, gf_ref,
    ogp, actp, gact, hid, gh, act_t, og_sh,
    acc_qkv, acc_gain, acc_out,
    e_s, e_r, e_b, e_br, e_g,
    l_s, l_r, l_b, l_br, l_g,
    isem, osem, snd, rcv, hsnd, hrcv, wsnd, wrcv,
):
    f = lax.axis_index("frame")
    r = lax.axis_index("row")
    core = lax.rem(f, 2)
    fx = f // 2
    y = r // 2
    zh = lax.rem(r, 2)
    a = y * 2 + core
    q = zh * 16 + fx

    def frame_peer(k):
        return lax.rem(f + k, NF)

    def a_peer(k):
        a2 = lax.rem(a + k, 8)
        return a2, (fx * 2 + lax.rem(a2, 2), (a2 // 2) * 2 + zh)

    def q_device(q2):
        return (lax.rem(q2, 16) * 2 + core, y * 2 + q2 // 16)

    barrier = pltpu.get_barrier_semaphore()

    fetches = [
        pltpu.make_async_copy(src, dst, isem.at[k])
        for k, (src, dst) in enumerate([
            (x_hbm, x_ref), (gain_hbm, gain_ref), (wqkv_hbm, wqkv_ref), (wout_hbm, wout_ref),
            (wconv_hbm, wconv_ref), (og_hbm, ogp.at[pl.ds(W, PIX)]),
        ])
    ]
    for fetch in fetches:
        fetch.start()

    @pl.loop(1, NF, unroll=True)
    def _(k):
        pl.semaphore_signal(barrier, inc=1, device_id=(frame_peer(k), r), device_id_type=MESH)

    @pl.loop(0, 16, unroll=True)
    def _(k):
        pl.semaphore_signal(barrier, inc=1, device_id=(k * 2 + core, y * 2 + 1 - zh), device_id_type=MESH)

    @pl.loop(2, 8, unroll=True)
    def _(k):
        a2 = lax.rem(y * 2 + k, 8)
        pl.semaphore_signal(
            barrier, inc=1, device_id=(fx * 2 + lax.rem(a2, 2), (a2 // 2) * 2 + zh), device_id_type=MESH)

    @pl.when(r > 0)
    def _():
        pl.semaphore_signal(barrier, inc=1, device_id=(f, r - 1), device_id_type=MESH)

    @pl.when(r < NR - 1)
    def _():
        pl.semaphore_signal(barrier, inc=1, device_id=(f, r + 1), device_id_type=MESH)

    col = lax.broadcasted_iota(jnp.int32, (W, C), 0)
    first_col = col == 0
    last_col = col == W - 1

    def after(z):
        return jnp.where(last_col, 0.0, pltpu.roll(z, W - 1, 0))

    def before(z):
        return jnp.where(first_col, 0.0, pltpu.roll(z, 1, 0))

    def shift_row(row):
        here = rows_of(row * W, W)
        own = ogp[here, :]
        wide = own.astype(F32)
        og_sh[here, :] = jnp.concatenate([after(wide).astype(BF16), own, before(wide).astype(BF16)], axis=1)

    def grad_act_row(row):
        total = jnp.zeros((W, 3 * C), F32)
        for i in range(3):
            total = total + nt(ogp[rows_of((row + 2 - i) * W, W), :], wconv_ref[i])
        gact[rows_of(row * W, W), :] = (
            after(total[:, :C]) + total[:, C : 2 * C] + before(total[:, 2 * C :]))

    for fetch in fetches:
        fetch.wait()

    @pl.loop(1, ROWS - 1)
    def _(row):
        grad_act_row(row)

    @pl.loop(1, ROWS + 1)
    def _(row):
        shift_row(row)

    pl.semaphore_wait(barrier, 31 + 16 + 6 + jnp.where(r > 0, 1, 0) + jnp.where(r < NR - 1, 1, 0))

    def to_time(phase, c, src, dst):
        @pl.loop(1, NF, unroll=True)
        def _(k):
            d = frame_peer(k)
            pltpu.make_async_remote_copy(
                src.at[rows_of(c * CP + d * M, M)], dst.at[rows_of(c * CP + f * M, M)],
                snd.at[phase, c], rcv.at[phase, c], device_id=(d, r), device_id_type=MESH,
            ).start()

        own = rows_of(c * CP + f * M, M)
        dst[own, :] = src[own, :]

    def arrived(phase, c, dst):
        view = dst.at[pl.ds(pl.multiple_of(c * CP, M), (NF - 1) * M)]
        pltpu.make_async_copy(view, view, rcv.at[phase, c]).wait()

    def left(phase, c, src):
        view = src.at[pl.ds(pl.multiple_of(c * CP, M), (NF - 1) * M)]
        pltpu.make_async_copy(view, view, snd.at[phase, c]).wait()

    def turn(t):
        return lax.rem(NC + 1 - t, NC)

    @pl.loop(0, NC)
    def _(t):
        to_time(0, turn(t), x_ref, xt)

    def halo_up(buf, s, piece):
        return pltpu.make_async_remote_copy(
            buf.at[pl.ds(W + piece * C, C)], buf.at[pl.ds(5 * W + piece * C, C)],
            hsnd.at[s, 0, piece], hrcv.at[s, 0, piece], device_id=(f, r - 1), device_id_type=MESH)

    def halo_down(buf, s, piece):
        return pltpu.make_async_remote_copy(
            buf.at[pl.ds(4 * W + piece * C, C)], buf.at[pl.ds(piece * C, C)],
            hsnd.at[s, 1, piece], hrcv.at[s, 1, piece], device_id=(f, r + 1), device_id_type=MESH)

    def halo_start(buf, s, pieces):
        @pl.when(r > 0)
        def _():
            for piece in pieces:
                halo_up(buf, s, piece).start()

        @pl.when(r < NR - 1)
        def _():
            for piece in pieces:
                halo_down(buf, s, piece).start()

    edge = jnp.zeros((W, C), BF16)

    @pl.when(r == 0)
    def _():
        ogp[pl.ds(0, W), :] = edge
        actp[pl.ds(0, W), :] = edge

    @pl.when(r == NR - 1)
    def _():
        ogp[pl.ds(5 * W, W), :] = edge
        actp[pl.ds(5 * W, W), :] = edge

    def halo_wait(buf, s):
        @pl.when(r > 0)
        def _():
            for piece in range(3):
                halo_up(buf, s, piece).wait_send()
                halo_down(buf, s, piece).wait_recv()

        @pl.when(r < NR - 1)
        def _():
            for piece in range(3):
                halo_down(buf, s, piece).wait_send()
                halo_up(buf, s, piece).wait_recv()

    gain = gain_ref[...]
    wcat = jnp.concatenate([wqkv_ref[0], wqkv_ref[1], wqkv_ref[2]], axis=1)
    scale = D ** (-0.5)
    sub = lax.broadcasted_iota(jnp.int32, (8, 2 * Q), 0)
    lane = lax.broadcasted_iota(jnp.int32, (8, 2 * Q), 1)
    diag = (lax.rem(sub, 4) == lax.rem(lane, 4)).astype(F32)
    first_half = lax.broadcasted_iota(jnp.int32, (NF // 2, 8, C), 1) < 4

    def quads(rows):
        lo, hi = rows[: NF // 2], rows[NF // 2 :]
        one = jnp.where(first_half, lo, pltpu.roll(hi, 4, 1)).reshape(Q, C)
        two = jnp.where(first_half, pltpu.roll(lo, 4, 1), hi).reshape(Q, C)
        return jnp.concatenate([one, two], axis=0).astype(BF16)

    def from_quads(rows):
        one = rows[:Q].reshape(NF // 2, 8, C)
        two = rows[Q:].reshape(NF // 2, 8, C)
        lo = jnp.where(first_half, one, pltpu.roll(two, 4, 1))
        hi = jnp.where(first_half, pltpu.roll(one, 4, 1), two)
        return jnp.concatenate([lo, hi], axis=0)

    def two_heads(tr, pair):
        wide = []
        for h in (2 * pair, 2 * pair + 1):
            pieces = [jnp.zeros((h * D, Q), BF16)] if h else []
            pieces.append(tr[h * D : (h + 1) * D])
            if h < HEADS - 1:
                pieces.append(jnp.zeros((C - (h + 1) * D, Q), BF16))
            wide.append(jnp.concatenate(pieces, axis=0))
        return jnp.concatenate(wide, axis=1)

    def by_head(rows):
        return jnp.concatenate([rows * head_of[h] for h in range(HEADS)], axis=0)

    chan = lax.broadcasted_iota(jnp.int32, (1, C), 1) // D
    head_of = [(chan == h).astype(BF16) for h in range(HEADS)]

    acc_qkv[...] = jnp.zeros_like(acc_qkv)
    acc_gain[...] = jnp.zeros_like(acc_gain)
    acc_out[...] = jnp.zeros_like(acc_out)

    @pl.loop(0, NC)
    def _(t):
        c = turn(t)
        arrived(0, c, xt)

        @pl.when(t == 0)
        def _():
            halo_start(ogp, 0, OG_PIECES[0])

        chunk = rows_of(c * CP, CP)
        unit, _ = normalize(xt[chunk, :].astype(F32))
        unit_t[chunk, :] = unit
        stage[...] = (unit * gain).reshape(NF, M, C)

        @pl.loop(0, NG)
        def _(j):
            g = c * NG + j
            eight = pl.ds(pl.multiple_of(j * 8, 8), 8)
            normed = quads(stage[:, eight, :])
            n_s[g] = normed
            qkv = nn(normed, wcat).astype(BF16)
            queries, keys, values = qkv[:, :C], qkv[:, C : 2 * C], qkv[:, 2 * C :]
            q_s[g] = queries
            v_s[g] = values
            q_tr = jnp.transpose(queries)
            k_tr = jnp.transpose(keys)
            v_tr = jnp.transpose(values)
            k_t[g] = k_tr
            mixed = []
            for b in range(2):
                at = slice(b * Q, (b + 1) * Q)
                parts = []
                for pair in range(HEADS // 2):
                    s = nn(keys[at], two_heads(q_tr[:, at], pair)).reshape(Q // 8, 8, 2 * Q)
                    top = jnp.max(s, axis=0)
                    top = jnp.maximum(top, pltpu.roll(top, 4, 0))
                    e = jnp.exp2((s - top[None]) * (scale * LOG2E))
                    below = jnp.sum(e, axis=0)
                    inv = diag / (below + pltpu.roll(below, 4, 0))
                    p = (e * inv[None]).reshape(Q, 2 * Q)
                    probs[(g * 2 + b) * 2 + pair] = p
                    pb = p.astype(BF16)
                    for k in range(2):
                        h = 2 * pair + k
                        parts.append(nn(v_tr[h * D : (h + 1) * D, at], pb[:, k * Q : (k + 1) * Q]))
                mixed.append(jnp.concatenate(parts, axis=0))
            stage[:, eight, :] = from_quads(jnp.transpose(jnp.concatenate(mixed, axis=1)))

        mix_s[chunk, :] = stage[...].reshape(CP, C).astype(BF16)
        to_time(1, c, mix_s, mix_f)

        for late in (1, 2):
            if OG_PIECES[late]:
                @pl.when(t == late - 1)
                def _(late=late):
                    halo_start(ogp, 0, OG_PIECES[late])

    def middle(c):
        arrived(1, c, mix_f)
        chunk = pl.ds(c * CP, CP)
        mixed = mix_f[chunk, :]
        hidden = x_ref[chunk, :].astype(F32) + nn(mixed, wout_ref[...])
        sigma = 1.0 / (1.0 + jnp.exp(-hidden))
        act = (hidden * sigma).astype(BF16)
        ghidden = (ogp[pl.ds(W + c * CP, CP), :].astype(F32)
                   + gact[chunk, :] * sigma * (1.0 + hidden * (1.0 - sigma)))
        ghb = ghidden.astype(BF16)
        gm_s[chunk, :] = nt(ghb, wout_ref[...]).astype(BF16)
        to_time(2, c, gm_s, gm_t)
        hid[chunk, :] = hidden
        actp[pl.ds(W + c * CP, CP), :] = act
        gh[chunk, :] = ghidden
        acc_out[...] += tn(mixed, ghb)
        act_t[:, c * CP : (c + 1) * CP] = jnp.transpose(act)

    middle(1)
    halo_wait(ogp, 0)

    @pl.loop(0, 2)
    def _(k):
        grad_act_row(k * (ROWS - 1))

    middle(0)
    middle(2)

    def sum_a_send(s, size, src, dst):
        @pl.loop(1, 8)
        def _(k):
            a2, dev = a_peer(k)
            pltpu.make_async_remote_copy(
                src.at[rows_of(a2 * size, size)], dst.at[rows_of(a * size, size)],
                wsnd.at[s], wrcv.at[s], device_id=dev, device_id_type=MESH).start()

        own = rows_of(a * size, size)
        dst[own, :] = src[own, :]

    def sum_b_send(s, size, base, src, mid, dst):
        view = src.at[pl.ds(0, 7 * size)]
        pltpu.make_async_copy(view, view, wrcv.at[s - 1]).wait()
        total = src[pl.ds(0, size), :].astype(F32)
        for k in range(1, 8):
            total = total + src[pl.ds(k * size, size), :].astype(F32)
        mid[...] = total.astype(BF16)

        @pl.loop(0, size // 16)
        def _(o):
            owner = 2 * (base + o)

            @pl.when(owner != q)
            def _():
                pltpu.make_async_remote_copy(
                    mid.at[rows_of(o * 16, 16)], dst.at[rows_of(q * 16, 16)],
                    wsnd.at[s], wrcv.at[s], device_id=q_device(owner), device_id_type=MESH).start()

            @pl.when(owner == q)
            def _():
                dst[rows_of(q * 16, 16), :] = mid[rows_of(o * 16, 16), :]

    def owns(size, base):
        return jnp.logical_and(
            lax.rem(q, 2) == 0, jnp.logical_and(q >= 2 * base, q < 2 * base + size // 8))

    def sum_b_back(s, size, base, src, dst):
        @pl.when(owns(size, base))
        def _():
            view = src.at[pl.ds(0, 31 * 16)]
            pltpu.make_async_copy(view, view, wrcv.at[s - 1]).wait()
            total = jnp.sum(src[...].astype(F32).reshape(32, 16, C), axis=0) * factor
            mine = rows_of((q // 2 - base) * 16, 16)
            dst[mine, :] = total.astype(BF16)

            @pl.loop(1, 32)
            def _(k):
                pltpu.make_async_remote_copy(
                    dst.at[mine], dst.at[mine], wsnd.at[s], wrcv.at[s],
                    device_id=q_device(lax.rem(q + k, 32)), device_id_type=MESH).start()

    def sum_a_back(s, size, base, src, dst):
        nblock = size // 16

        @pl.when(owns(size, base))
        def _():
            view = src.at[pl.ds(0, (nblock - 1) * 16)]
            pltpu.make_async_copy(view, view, wrcv.at[s - 1]).wait()

        @pl.when(jnp.logical_not(owns(size, base)))
        def _():
            view = src.at[pl.ds(0, nblock * 16)]
            pltpu.make_async_copy(view, view, wrcv.at[s - 1]).wait()

        own = rows_of(a * size, size)

        @pl.loop(1, 8)
        def _(k):
            pltpu.make_async_remote_copy(
                src, dst.at[own], wsnd.at[s], wrcv.at[s], device_id=a_peer(k)[1], device_id_type=MESH).start()

        pltpu.make_async_copy(src, dst.at[own], osem.at[s // 4]).start()

    def sum_finish(s, size, base, src, mid, back, total, dst):
        own = rows_of(a * size, size)
        pltpu.make_async_copy(total, dst.at[own], osem.at[s // 4]).wait()
        view = dst.at[pl.ds(0, 7 * size)]
        pltpu.make_async_copy(view, view, wrcv.at[s + 3]).wait()
        sent = src.at[pl.ds(0, 7 * size)]
        pltpu.make_async_copy(sent, sent, wsnd.at[s]).wait()
        nblock = size // 16

        @pl.when(owns(size, base))
        def _():
            few = mid.at[pl.ds(0, (nblock - 1) * 16)]
            pltpu.make_async_copy(few, few, wsnd.at[s + 1]).wait()
            many = back.at[pl.ds(0, 31 * 16)]
            pltpu.make_async_copy(many, many, wsnd.at[s + 2]).wait()

        @pl.when(jnp.logical_not(owns(size, base)))
        def _():
            few = mid.at[pl.ds(0, nblock * 16)]
            pltpu.make_async_copy(few, few, wsnd.at[s + 1]).wait()

        pltpu.make_async_copy(view, view, wsnd.at[s + 3]).wait()

    @pl.loop(0, 2)
    def _(k):
        shift_row(k * (ROWS + 1))

    for i in range(3):
        grad = nn(act_t[...], og_sh[(2 - i) * W : (2 - i) * W + PIX, :])
        for j in range(3):
            at = (3 * i + j) * C
            e_s[at : at + C, :] = grad[:, j * C : (j + 1) * C].astype(BF16)
    e_s[9 * C : 10 * C, :] = acc_out[...].astype(BF16)

    def conv_row(row):
        total = jnp.zeros((W, 3 * C), F32)
        for i in range(3):
            wide = jnp.concatenate([wconv_ref[i, j * C : (j + 1) * C, :] for j in range(3)], axis=1)
            total = total + nn(actp[rows_of((row + i) * W, W), :], wide)
        here = rows_of(row * W, W)
        conv = before(total[:, :C]) + total[:, C : 2 * C] + after(total[:, 2 * C :])
        out_ref[here, :] = (hid[here, :] + conv).astype(BF16)

    @pl.loop(0, NC)
    def _(t):
        c = turn(t)
        arrived(2, c, gm_t)
        chunk = rows_of(c * CP, CP)
        stage[...] = gm_t[chunk, :].astype(F32).reshape(NF, M, C)

        @pl.loop(0, NG)
        def _(j):
            g = c * NG + j
            eight = pl.ds(pl.multiple_of(j * 8, 8), 8)
            gmixed = quads(stage[:, eight, :])
            gm_tr = jnp.transpose(gmixed)
            queries, values, k_tr = q_s[g], v_s[g], k_t[g]
            gqs, gks, gvs = [], [], []
            for b in range(2):
                at = slice(b * Q, (b + 1) * Q)
                parts, scores, weights = [], [], []
                for pair in range(HEADS // 2):
                    gp = nn(values[at], two_heads(gm_tr[:, at], pair)).reshape(Q // 8, 8, 2 * Q)
                    p = probs[(g * 2 + b) * 2 + pair]
                    p3 = p.reshape(Q // 8, 8, 2 * Q)
                    dot = jnp.sum(p3 * gp, axis=0)
                    dot = dot + pltpu.roll(dot, 4, 0)
                    gs = (p3 * (gp - dot[None]) * scale).reshape(Q, 2 * Q).astype(BF16)
                    for k in range(2):
                        h = 2 * pair + k
                        parts.append(nn(k_tr[h * D : (h + 1) * D, at], gs[:, k * Q : (k + 1) * Q]))
                    scores.append(gs)
                    weights.append(p.astype(BF16))
                gqs.append(jnp.concatenate(parts, axis=0))
                gks.append(nn(jnp.concatenate(scores, axis=1), by_head(queries[at])))
                gvs.append(nn(jnp.concatenate(weights, axis=1), by_head(gmixed[at])))
            gq = jnp.transpose(jnp.concatenate(gqs, axis=1))
            gk, gv = jnp.concatenate(gks, axis=0), jnp.concatenate(gvs, axis=0)
            grads = jnp.concatenate([gq.astype(BF16), gk.astype(BF16), gv.astype(BF16)], axis=1)
            stage[:, eight, :] = from_quads(nt(grads, wcat))
            acc_qkv[...] += tn(n_s[g], grads)

        gnormed = stage[...].reshape(CP, C).astype(BF16)
        gn_s[chunk, :] = gnormed
        to_time(3, c, gn_s, gn_f)
        @pl.when(t == 0)
        def _():
            sum_a_send(0, EP, e_s, e_r)

        acc_gain[...] += jnp.sum((gnormed.astype(F32) * unit_t[chunk, :]).reshape(CP // 8, 8, C), axis=0)


    for i in range(3):
        for k in range(8):
            lo = max(i * C, k * 48)
            hi = min((i + 1) * C, (k + 1) * 48)
            if lo < hi:
                at = k * LP + lo - k * 48
                l_s[at : at + hi - lo, :] = acc_qkv[lo - i * C : hi - i * C, i * C : (i + 1) * C].astype(BF16)
    total_gain = jnp.sum(acc_gain[...], axis=0, keepdims=True)
    for k in range(8):
        l_s[k * LP + 48 : (k + 1) * LP, :] = jnp.broadcast_to(total_gain, (16, C)).astype(BF16)
    sum_a_send(4, LP, l_s, l_r)
    halo_start(actp, 1, ACT_PIECES[0])

    def put_out(k, at, size):
        rows = pl.ds(at, size)
        return pltpu.make_async_copy(out_ref.at[rows], out_hbm.at[rows], osem.at[2 + k])

    @pl.loop(1, ROWS - 1)
    def _(row):
        conv_row(row)

    put_out(0, W, 2 * W).start()
    def put_gf(c):
        chunk = rows_of(c * CP, CP)
        return pltpu.make_async_copy(gf_ref.at[chunk], gf_hbm.at[chunk], osem.at[5 + c])

    def grad_frames(c):
        arrived(3, c, gn_f)
        chunk = rows_of(c * CP, CP)
        unit, inverse = normalize(x_ref[chunk, :].astype(F32))
        gscaled = gn_f[chunk, :].astype(F32) * gain
        first = jnp.mean(gscaled, axis=-1, keepdims=True)
        second = jnp.mean(gscaled * unit, axis=-1, keepdims=True)
        gf_ref[chunk, :] = (gh[chunk, :] + inverse * (gscaled - first - unit * second)).astype(BF16)
        put_gf(c).start()

    grad_frames(1)
    sum_b_send(5, LP, EB, l_r, l_b, l_br)
    sum_b_send(1, EP, 0, e_r, e_b, e_br)
    halo_start(actp, 1, ACT_PIECES[1])

    grad_frames(0)
    sum_b_back(6, LP, EB, l_br, l_g)
    sum_b_back(2, EP, 0, e_br, e_g)
    halo_start(actp, 1, ACT_PIECES[2])
    grad_frames(2)
    sum_a_back(7, LP, EB, l_g, l_f)
    sum_a_back(3, EP, 0, e_g, e_f)
    halo_wait(actp, 1)

    @pl.loop(0, 2)
    def _(k):
        conv_row(k * (ROWS - 1))

    put_out(1, 0, W).start()
    put_out(2, 3 * W, W).start()
    sum_finish(0, EP, 0, e_r, e_b, e_br, e_g, e_f)

    @pl.loop(0, NC)
    def _(c):
        left(0, c, x_ref)
        left(1, c, mix_s)
        left(2, c, gm_s)
        left(3, c, gn_s)

    for c in range(NC):
        put_gf(c).wait()
    put_out(0, W, 2 * W).wait()
    put_out(1, 0, W).wait()
    put_out(2, 3 * W, W).wait()
    sum_finish(4, LP, EB, l_r, l_b, l_br, l_g, l_f)


def finish(
    out_s, gf_s, e_h, l_h, out_h, gf_h, gain_h, qkv_h, gout_h, conv_h,
    gain, qkv, gout, conv, e_v, l_v, out_v, gf_v, sem,
):
    def put(k, src, dst):
        copy = pltpu.make_async_copy(src, dst, sem.at[k])
        copy.start()
        return copy

    early, late = put(6, e_h, e_v), put(7, l_h, l_v)
    first, second = put(8, out_s, out_v), put(9, gf_s, gf_v)
    copies = []
    early.wait()
    conv[...] = e_v[: 9 * C, :].astype(F32)
    copies.append(put(2, conv, conv_h))
    gout[...] = e_v[9 * C :, :].astype(F32)
    copies.append(put(3, gout, gout_h))
    first.wait()
    copies.append(put(0, out_v, out_h))
    second.wait()
    copies.append(put(1, gf_v, gf_h))
    late.wait()
    for k in range(8):
        qkv[k * 48 : (k + 1) * 48, :] = l_v[k * LP : k * LP + 48, :].astype(F32)
    copies.append(put(4, qkv, qkv_h))
    gain[...] = l_v[48:64, :].astype(F32)[:1]
    copies.append(put(5, gain, gain_h))
    for copy in copies:
        copy.wait()


def on_device(frames, norm_gain, qkv_weight, out_weight, conv_weight, out_grad):
    total_pixels = PIX * NF * NR
    factor = 1.0 / math.sqrt(total_pixels)
    hbm = pl.BlockSpec(memory_space=pltpu.HBM)
    sds = jax.ShapeDtypeStruct
    full = (PIX, C)
    parts = pl.pallas_call(
        lambda *refs: kernel(factor, *refs),
        out_shape=(sds(full, BF16), sds(full, BF16), sds((8 * EP, C), BF16), sds((8 * LP, C), BF16)),
        in_specs=[hbm] * 6,
        out_specs=(hbm,) * 4,
        scratch_shapes=[
            pltpu.VMEM(full, BF16),
            pltpu.VMEM((1, C), F32),
            pltpu.VMEM((3, C, C), BF16),
            pltpu.VMEM((C, C), BF16),
            pltpu.VMEM((3, 3 * C, C), BF16),
            pltpu.VMEM(full, BF16),
            pltpu.VMEM(full, F32),
            pltpu.VMEM((NF, M, C), F32),
            pltpu.VMEM((NC * NG, C, G), BF16),
            pltpu.VMEM((NC * NG, G, C), BF16),
            pltpu.VMEM((NC * NG, G, C), BF16),
            pltpu.VMEM((NC * NG, G, C), BF16),
            pltpu.VMEM((NC * NG * HEADS, Q, 2 * Q), F32),
            pltpu.VMEM(full, BF16),
            pltpu.VMEM(full, BF16),
            pltpu.VMEM(full, BF16),
            pltpu.VMEM(full, BF16),
            pltpu.VMEM(full, BF16),
            pltpu.VMEM(full, BF16),
            pltpu.VMEM(full, BF16),
            pltpu.VMEM(full, BF16),
            pltpu.VMEM((PIX + 2 * W, C), BF16),
            pltpu.VMEM((PIX + 2 * W, C), BF16),
            pltpu.VMEM(full, F32),
            pltpu.VMEM(full, F32),
            pltpu.VMEM(full, F32),
            pltpu.VMEM((C, PIX), BF16),
            pltpu.VMEM((PIX + 2 * W, 3 * C), BF16),
            pltpu.VMEM((C, 3 * C), F32),
            pltpu.VMEM((8, C), F32),
            pltpu.VMEM((C, C), F32),
            pltpu.VMEM((8 * EP, C), BF16),
            pltpu.VMEM((8 * EP, C), BF16),
            pltpu.VMEM((EP, C), BF16),
            pltpu.VMEM((32 * 16, C), BF16),
            pltpu.VMEM((EP, C), BF16),
            pltpu.VMEM((8 * LP, C), BF16),
            pltpu.VMEM((8 * LP, C), BF16),
            pltpu.VMEM((LP, C), BF16),
            pltpu.VMEM((32 * 16, C), BF16),
            pltpu.VMEM((LP, C), BF16),
            pltpu.SemaphoreType.DMA((6,)),
            pltpu.SemaphoreType.DMA((8,)),
            pltpu.SemaphoreType.DMA((4, NC)),
            pltpu.SemaphoreType.DMA((4, NC)),
            pltpu.SemaphoreType.DMA((2, 2, 3)),
            pltpu.SemaphoreType.DMA((2, 2, 3)),
            pltpu.SemaphoreType.DMA((8,)),
            pltpu.SemaphoreType.DMA((8,)),
        ],
        compiler_params=pltpu.CompilerParams(
            collective_id=0, has_side_effects=True, vmem_limit_bytes=60 << 20
        ),
        name="block",
    )(
        frames.reshape(full),
        norm_gain.reshape(1, C),
        qkv_weight,
        out_weight,
        conv_weight.reshape(3, 3 * C, C),
        out_grad.reshape(full),
    )
    sizes = (sds(full, BF16), sds(full, BF16), sds((1, C), F32),
             sds((3 * C, C), F32), sds((C, C), F32), sds((9 * C, C), F32))
    outs = pl.pallas_call(
        finish,
        out_shape=sizes,
        in_specs=[hbm] * 4,
        out_specs=(hbm,) * 6,
        scratch_shapes=[pltpu.VMEM(s.shape, F32) for s in sizes[2:]] + [
            pltpu.VMEM((8 * EP, C), BF16), pltpu.VMEM((8 * LP, C), BF16),
            pltpu.VMEM(full, BF16), pltpu.VMEM(full, BF16), pltpu.SemaphoreType.DMA((10,))],
        compiler_params=pltpu.CompilerParams(vmem_limit_bytes=60 << 20),
        name="finish",
    )(*parts)
    output, grad_frames, grad_gain, grad_qkv, grad_out, grad_conv = outs
    return (
        output.reshape(frames.shape),
        grad_frames.reshape(frames.shape),
        grad_gain.reshape(C),
        grad_qkv.reshape(3, C, C),
        grad_out,
        grad_conv.reshape(3, 3, C, C),
    )


def solution(mesh):
    return jax.shard_map(
        on_device,
        mesh=mesh,
        in_specs=(P("frame", "row", None, None), P(), P(), P(), P(), P("frame", "row", None, None)),
        out_specs=(
            P("frame", "row", None, None),
            P("frame", "row", None, None),
            P(),
            P(),
            P(),
            P(),
        ),
        check_vma=False,
    )
```
